512 devices in a mesh: stem: 8 (over x, y_hi), tm: 64 (over z, y_lo, core).
Axes of the slice: x: 4, y: 8 (y_hi: 2, y_lo: 4; y = y_hi * 4 + y_lo), z: 8, core: 2. Of those that a mesh axis runs over, the one named last changes fastest.
Arguments:
- hidden: bfloat16 [8, 4096, 1024], P('stem', 'tm'), may hold values from -3 to 3
- control_ids: int32 [4096], P('tm'), may hold values from 0 to 127
- control_table: bfloat16 [128, 1024], replicated, may hold values from -3 to 3
- activity: int32 [8, 32], P('stem'), may hold values from 0 to 1, as said below
- ada: float32 [8, 3, 1024], P('stem'), may hold values from -4 to 4
- w_qkv: bfloat16 [1024, 1536], replicated, may hold values from -1 to 1
- w_out: bfloat16 [512, 1024], replicated, may hold values from -0.25 to 0.25
Outputs:
- block_out: bfloat16 [8, 4096, 1024], P('stem', 'tm')
The draws below stay inside these ranges and needn't reach their ends.
Inputs may be any that keep to these rules, and one draw needn't show every extreme that they name: `activity`: 1 marks an active bar of a stem, 0 a silent one.
All inputs are finite; a program needn't handle non-finite values.
Results may differ from the reference program's by a relative error of at most 0.019.
Values may be sent and summed in bfloat16 or wider, within the bound.
A program may use at most 64 MiB of HBM per device.

```python
import math
import jax
import jax.numpy as jnp
import numpy as np
from jax import lax

D = 1024
HEADS = 8
HEAD_DIM = 64
INNER = 512
CVOCAB = 128
BAR = 128
FRAMES = 4096
BARS = 32
STEMS = 8


def draw_activity(key, part):
    key = jax.random.fold_in(key, 11)
    first_key, second_key = jax.random.split(key)
    threshold = jax.random.randint(first_key, (STEMS, 1), 1, 8)
    rolled = jax.random.randint(second_key, (STEMS, BARS), 0, 8)
    return (rolled < threshold).astype(jnp.int32)


def draw_w_qkv(key, part):
    key = jax.random.fold_in(key, 7)
    base = jnp.clip(jax.random.normal(key, (D, 3 * INNER), jnp.float32), -6.0, 6.0) * D ** (-0.5)
    return base.astype(jnp.bfloat16)


def with_ends(entries, stream_key, least, high):
    shape = entries.shape
    place = [jax.random.randint(jax.random.fold_in(stream_key, axis), (), 0, shape[axis]) for axis in range(len(shape))]
    entries = entries.at[tuple(place)].set(least)
    longest = shape.index(max(shape))
    place[longest] = (place[longest] + 1) % shape[longest]
    return entries.at[tuple(place)].set(high)


def block_levels(stream_key, shape, pieces, least, largest):
    loudness, own = 1.0, jax.random.fold_in(stream_key, 6)
    for position, parts in pieces:
        steps = jnp.exp(jax.random.uniform(jax.random.fold_in(own, position), (parts,), jnp.float32, least / len(pieces), largest / len(pieces)))
        loudness = loudness * jnp.repeat(steps, shape[position] // parts).reshape([-1 if axis == position else 1 for axis in range(len(shape))])
    return loudness


def rank_bounds(number_of, slope):
    loads = [(1 << 20) // math.isqrt(rank ** slope) + 1 for rank in range(1, number_of + 1)]
    deviation = 1 + sum(loads) // (1 << 30)
    return np.cumsum(np.array([max(1, weight // deviation) for weight in loads]))


def ranked_ids(rng, extent, number_of, skew):
    grid = rank_bounds(number_of, skew)
    pick = jax.random.randint(jax.random.fold_in(rng, 1), extent, 0, int(grid[number_of - 1]))
    standing = jnp.searchsorted(jnp.asarray(grid, jnp.int32), pick, side="right")
    return jax.random.permutation(jax.random.fold_in(rng, 2), number_of)[standing].astype(jnp.int32)


def gaussian(rng, extent, spread, bound, pieces=(), kind=jnp.bfloat16):
    level = block_levels(rng, extent, pieces, -0.22, 0.18) if pieces else 1.0
    drawn = jax.random.normal(rng, extent, jnp.float32) * spread * level
    return jnp.minimum(jnp.maximum(drawn, -bound), bound).astype(kind)


def setup_inputs(seed: int = 0) -> dict:
    splits = jax.random.split(jax.random.key(seed), 8)
    return {
        "hidden": gaussian(splits[0], (STEMS, FRAMES, D), 0.5, 3.0, ((0, 8), (1, 64))),
        "control_ids": with_ends(ranked_ids(splits[1], (FRAMES,), CVOCAB, 2), jax.random.fold_in(splits[1], 3), 0, CVOCAB - 1).astype(jnp.int32),
        "control_table": gaussian(splits[2], (CVOCAB, D), 0.5, 3.0),
        "activity": draw_activity(jax.random.fold_in(splits[7], 71), 0),
        "ada": gaussian(splits[4], (STEMS, 3, D), 1.0, 4.0, ((0, 8),), jnp.float32),
        "w_qkv": draw_w_qkv(jax.random.fold_in(splits[7], 71), 0),
        "w_out": gaussian(splits[6], (INNER, D), INNER ** -0.5, 0.25),
    }


epsilon = 1e-06

def reference(hidden, control_ids, control_table, activity, ada, w_qkv, w_out):
    stem_count, frames, features = hidden.shape
    inner_width = w_out.shape[0]
    lookup = jnp.take(control_table, control_ids, axis=0).astype(jnp.float32)
    residual = hidden.astype(jnp.float32) + lookup[None]
    row_mean = lax.optimization_barrier(jnp.mean(residual, axis=-1, keepdims=True))
    row_var = lax.optimization_barrier(jnp.mean(jnp.square(residual - row_mean), axis=-1, keepdims=True))
    normed = ((residual - row_mean) * lax.rsqrt(row_var + epsilon) * (1.0 + ada[:, 1][:, None, :]) + ada[:, 0][:, None, :]).astype(jnp.bfloat16)
    projected = jnp.dot(normed.reshape(-1, features), w_qkv, preferred_element_type=jnp.float32).astype(jnp.bfloat16)
    projected = projected.reshape(stem_count, frames, 3, HEADS, HEAD_DIM)
    queries = projected[:, :, 0]
    key_rows = projected[:, :, 1]
    value_rows = projected[:, :, 2]
    score_scale = 1.0 / math.sqrt(HEAD_DIM)
    stem_scores = jnp.einsum('sqhd,tqhd->sqht', queries.astype(jnp.float32), key_rows.astype(jnp.float32)) * score_scale
    value_across = jnp.transpose(value_rows, (1, 0, 2, 3))
    bar_of = jnp.arange(frames, dtype=jnp.int32) // BAR
    live = jnp.take(activity, bar_of, axis=1) > 0
    block_len = math.gcd(frames, 512)
    block_count = frames // block_len
    all_frames = jnp.arange(frames, dtype=jnp.int32)

    def per_stem(stem_slice):
        query_stem, key_stem, value_stem, score_stem, live_stem = stem_slice

        def per_block(block_index):
            first = (block_index * block_len).astype(jnp.int32)
            query_block = lax.dynamic_slice_in_dim(query_stem, first, block_len, 0)
            stem_block = lax.dynamic_slice_in_dim(score_stem, first, block_len, 0)
            across_block = lax.dynamic_slice_in_dim(value_across, first, block_len, 0)
            live_block = lax.dynamic_slice_in_dim(live_stem, first, block_len, 0)
            rows = first + jnp.arange(block_len, dtype=jnp.int32)
            allowed = live_block[:, None] & live_stem[None, :] & (rows[:, None] != all_frames[None, :])
            time_scores = jnp.einsum('qhd,khd->qhk', query_block.astype(jnp.float32), key_stem.astype(jnp.float32)) * score_scale
            time_scores = jnp.where(allowed[:, None, :], time_scores, -jnp.inf)
            row_max = jnp.maximum(lax.optimization_barrier(jnp.max(time_scores, axis=-1)), lax.optimization_barrier(jnp.max(stem_block, axis=-1)))
            time_weights = jnp.where(allowed[:, None, :], jnp.exp(time_scores - row_max[..., None]), 0.0)
            stem_weights = jnp.exp(stem_block - row_max[..., None])
            denominator = lax.optimization_barrier(jnp.sum(time_weights, axis=-1)) + lax.optimization_barrier(jnp.sum(stem_weights, axis=-1))
            numerator = jnp.einsum('qhk,khd->qhd', time_weights.astype(jnp.bfloat16).astype(jnp.float32), value_stem.astype(jnp.float32))
            numerator = numerator + jnp.einsum('qhs,qshd->qhd', stem_weights.astype(jnp.bfloat16).astype(jnp.float32), across_block.astype(jnp.float32))
            return (numerator / denominator[..., None]).astype(jnp.bfloat16).reshape(block_len, inner_width)
        return lax.map(per_block, jnp.arange(block_count, dtype=jnp.int32)).reshape(frames, inner_width)
    attended = lax.map(per_stem, (queries, key_rows, value_rows, stem_scores, live))
    branch = jnp.dot(attended.reshape(-1, inner_width), w_out, preferred_element_type=jnp.float32).reshape(stem_count, frames, features)
    return (residual + ada[:, 2][:, None, :] * branch).astype(jnp.bfloat16)
```

```python
import functools
import math

import jax
import jax.numpy as jnp
from jax import lax
from jax.experimental import pallas as pl
from jax.experimental.pallas import tpu as pltpu
from jax.sharding import PartitionSpec as P

MESH = pl.DeviceIdType.MESH
F32 = jnp.float32
BF16 = jnp.bfloat16
LOG2E = math.log2(math.e)
NEG = -1e30
FR = 64
LANES = 128
QT = 256


def lane_iota(rows):
    return lax.broadcasted_iota(jnp.int32, (rows, LANES), 1)


def swap_halves(x):
    return pltpu.roll(x, 64, 1)


def nt_dot(a, b):
    return lax.dot_general(a, b, (((1,), (1,)), ((), ())), preferred_element_type=F32)


def unfold_queries(folded, z_ref, row):
    f = folded.astype(F32)
    low = lane_iota(32) < 64
    z_ref[pl.ds(row, 32), :] = jnp.where(low, f, 0.0).astype(BF16)
    z_ref[pl.ds(row + 32, 32), :] = jnp.where(low, swap_halves(f), 0.0).astype(BF16)


def ones_values(kv):
    return jnp.where(lane_iota(kv.shape[0]) < 64, jnp.ones_like(kv), kv)


def pack_part(m, acc):
    rows = acc.shape[0]
    lane = lane_iota(rows)
    total = jnp.where(lane < 64, acc, swap_halves(acc))
    value = acc / total
    lse = m + jnp.log(total)
    hi = lse.astype(BF16).astype(F32)
    mid = (lse - hi).astype(BF16).astype(F32)
    lo = lse - hi - mid
    return jnp.where(
        lane < 16, hi, jnp.where(lane < 32, mid, jnp.where(lane < 64, lo, value))
    ).astype(BF16)


def unpack_lse(part):
    return part[:, 0:1] + part[:, 16:17] + part[:, 32:33]


def kernel(
    hidden_ref, ids_ref, table_ref, act_ref, ada_ref, wqkv_hbm, wout_hbm, out_ref,
    wqkv, wout, resid, sb, kvb, qb, zb, rst, zst, mb, accb, biasb, selfm, ob, so, rt, rs,
    w_sem, zk_s, zk_r, zq_s, zq_r, st_s, st_r, y_s, y_r, f_s, c_s, c_r, tb_s, tb_r, sb_s, sb_r,
):
    s = lax.axis_index("stem")
    t = lax.axis_index("tm")
    z = lax.div(t, 8)
    y = lax.rem(lax.div(t, 2), 4)
    c = lax.rem(t, 2)
    y1 = y + 1 - 2 * lax.rem(y, 2)
    inner = jnp.logical_or(y == 1, y == 2)
    innerx = jnp.where(inner, 1, 0)
    p2 = jnp.where(inner, 3 - y, 3 - y1)
    p3 = jnp.where(inner, 3 - y1, 3 - y)
    peers = (y1, p2, p3)

    def at(zz, yy, cc):
        return (s, (zz * 4 + yy) * 2 + cc)

    def zpeer(d):
        return lax.rem(z + d, 8)

    def speer(d):
        return lax.rem(s + d, 8)

    core = at(z, y, 1 - c)

    barrier = pltpu.get_barrier_semaphore()
    for d in range(1, 8):
        pl.semaphore_signal(barrier, inc=1, device_id=at(zpeer(d), y, c), device_id_type=MESH)
        pl.semaphore_signal(barrier, inc=1, device_id=(speer(d), t), device_id_type=MESH)
    for p in peers:
        pl.semaphore_signal(barrier, inc=1, device_id=at(z, p, c), device_id_type=MESH)
    pl.semaphore_signal(barrier, inc=1, device_id=core, device_id_type=MESH)

    def wcopy(i):
        if i == 3:
            return pltpu.make_async_copy(wout_hbm, wout, w_sem.at[3])
        cols = pl.ds(i * 512, 512)
        return pltpu.make_async_copy(wqkv_hbm.at[:, cols], wqkv.at[i], w_sem.at[i])

    for i in (1, 2, 0, 3):
        wcopy(i).start()

    onehot = (lax.broadcasted_iota(jnp.int32, (128, FR), 0) == ids_ref[...]).astype(BF16)
    lookup = lax.dot_general(
        onehot, table_ref[...], (((0,), (0,)), ((), ())), preferred_element_type=F32
    )
    residual = hidden_ref[...].astype(F32) + lookup
    resid[...] = residual
    mean = jnp.mean(residual, axis=-1, keepdims=True)
    cent = residual - mean
    var = jnp.mean(jnp.square(cent), axis=-1, keepdims=True)
    normed = (cent * lax.rsqrt(var + 1e-6) * (1.0 + ada_ref[1:2, :]) + ada_ref[0:1, :]).astype(BF16)

    low = lane_iota(FR) < 64
    wcopy(1).wait()
    keys = jnp.dot(normed, wqkv[1], preferred_element_type=F32)
    wcopy(2).wait()
    values = jnp.dot(normed, wqkv[2], preferred_element_type=F32)
    for j in range(4):
        k2 = keys[:, 128 * j : 128 * j + 128]
        v2 = values[:, 128 * j : 128 * j + 128]
        sb[2 * j, 0:64, :] = jnp.where(low, k2, swap_halves(v2)).astype(BF16)
        sb[2 * j + 1, 0:64, :] = jnp.where(low, swap_halves(k2), v2).astype(BF16)

    pl.semaphore_wait(barrier, 18)

    def zk_copy(d):
        return pltpu.make_async_remote_copy(
            src_ref=sb.at[zpeer(d), pl.ds(0, 64)],
            dst_ref=kvb.at[y, c, pl.ds(pl.multiple_of(z * 64, 64), 64)],
            send_sem=zk_s.at[d], recv_sem=zk_r.at[d],
            device_id=at(zpeer(d), y, c), device_id_type=MESH,
        )

    def zq_copy(d):
        return pltpu.make_async_remote_copy(
            src_ref=sb.at[zpeer(d), pl.ds(64, 32)],
            dst_ref=qb.at[z],
            send_sem=zq_s.at[d], recv_sem=zq_r.at[d],
            device_id=at(zpeer(d), y, c), device_id_type=MESH,
        )

    def st_copy(d):
        return pltpu.make_async_remote_copy(
            src_ref=sb.at[speer(d)], dst_ref=rst.at[s],
            send_sem=st_s.at[d], recv_sem=st_r.at[d],
            device_id=(speer(d), t), device_id_type=MESH,
        )

    order = (4, 3, 5, 2, 6, 1, 7)
    for d in order:
        zk_copy(d).start()

    wcopy(0).wait()
    queries = jnp.dot(normed, wqkv[0], preferred_element_type=F32).astype(BF16).astype(F32) * 0.125
    low32 = lane_iota(32) < 64
    for j in range(4):
        q2 = queries[:, 128 * j : 128 * j + 128]
        a, b = q2[0:32], q2[32:64]
        sb[2 * j, 64:96, :] = jnp.where(low32, a, swap_halves(b)).astype(BF16)
        sb[2 * j + 1, 64:96, :] = jnp.where(low32, swap_halves(a), b).astype(BF16)
    for d in order:
        zq_copy(d).start()
    for d in order:
        st_copy(d).start()

    kvb[y, c, pl.ds(pl.multiple_of(z * 64, 64), 64), :] = sb[z, 0:64, :]
    qb[z] = sb[z, 64:96, :]
    rst[s] = sb[s]
    group = lax.div(lax.broadcasted_iota(jnp.int32, (8, 512), 1), 64)
    for yy in range(4):
        row = jnp.zeros((8, 512), F32)
        for zz in range(8):
            bias = jnp.where(act_ref[0, zz * 4 + yy] > 0, 0.0, NEG).astype(F32)
            row = jnp.where(group == zz, bias, row)
        biasb[yy] = row
    for j in range(4):
        q2 = queries[:, 128 * j : 128 * j + 128]
        k2 = keys[:, 128 * j : 128 * j + 128].astype(BF16).astype(F32)
        prod = q2 * k2
        even = jnp.sum(jnp.where(low, prod, 0.0), axis=1, keepdims=True)
        odd = jnp.sum(jnp.where(low, 0.0, prod), axis=1, keepdims=True)
        selfm[2 * j] = jnp.broadcast_to(even, (FR, LANES))
        selfm[2 * j + 1] = jnp.broadcast_to(odd, (FR, LANES))

    for d in order[::-1]:
        zk_copy(d).wait_recv()

    def c_copy(i, yy):
        return pltpu.make_async_remote_copy(
            src_ref=kvb.at[yy, c], dst_ref=kvb.at[yy, c],
            send_sem=c_s.at[i], recv_sem=c_r.at[i], device_id=core, device_id_type=MESH,
        )

    def c_arrival(i, yy):
        return pltpu.make_async_remote_copy(
            src_ref=kvb.at[yy, 1 - c], dst_ref=kvb.at[yy, 1 - c],
            send_sem=c_s.at[i], recv_sem=c_r.at[i], device_id=core, device_id_type=MESH,
        )

    def y_copy(block, target, ssem, rsem):
        return pltpu.make_async_remote_copy(
            src_ref=kvb.at[block, c], dst_ref=kvb.at[block, c],
            send_sem=ssem, recv_sem=rsem, device_id=at(z, target, c), device_id_type=MESH,
        )

    send_near = y_copy(y, y1, y_s.at[0], y_r.at[0])
    send_far = y_copy(y, p2, y_s.at[1], y_r.at[2 - innerx])
    send_far.start()
    send_near.start()
    c_copy(0, y).start()

    for d in order[::-1]:
        zq_copy(d).wait_recv()
    for zz in range(8):
        unfold_queries(qb[zz], zb, zz * 64)

    def step(kv_ref, bias, first):
        kv = kv_ref[...]
        w = ones_values(kv)

        @pl.loop(0, 512 // QT)
        def _(i):
            rows = pl.ds(pl.multiple_of(i * QT, QT), QT)
            sc = nt_dot(zb[rows, :], kv) + bias
            top = jnp.max(sc, axis=1, keepdims=True)
            if first:
                m = jnp.broadcast_to(top, (QT, LANES))
            else:
                old = mb[rows, :]
                m = jnp.maximum(old, top)
            p = jnp.exp2((sc - m[:, 0:1]) * LOG2E).astype(BF16)
            new = jnp.dot(p, w, preferred_element_type=F32)
            if first:
                accb[rows, :] = new
            else:
                accb[rows, :] = accb[rows, :] * jnp.exp2((old - m) * LOG2E) + new
            mb[rows, :] = m

    step(kvb.at[y, c], biasb[y, 0:1, :], True)
    c_arrival(0, y).wait_recv()
    step(kvb.at[y, 1 - c], biasb[y, 0:1, :], False)

    for d in order[::-1]:
        st_copy(d).wait_recv()
    for ss in range(8):
        unfold_queries(rst[ss, 64:96, :], zst, ss * 64)
    kvst = jnp.concatenate([rst[ss, 0:64, :] for ss in range(8)], axis=0)
    wst = ones_values(kvst)
    col = lax.broadcasted_iota(jnp.int32, (QT, 512), 1)

    @pl.loop(0, 512 // QT)
    def _(i):
        row0 = pl.multiple_of(i * QT, QT)
        rows = pl.ds(row0, QT)
        row = lax.broadcasted_iota(jnp.int32, (QT, 512), 0) + row0
        keep = jnp.logical_and(jnp.bitwise_and(row, 63) == jnp.bitwise_and(col, 63), row != col)
        sc = jnp.where(keep, nt_dot(zst[rows, :], kvst), NEG)
        top = jnp.max(sc, axis=1, keepdims=True)
        p = jnp.exp2((sc - top) * LOG2E).astype(BF16)
        so[rows, :] = pack_part(top, jnp.dot(p, wst, preferred_element_type=F32))

    def sb_copy(d):
        return pltpu.make_async_remote_copy(
            src_ref=so.at[pl.ds(pl.multiple_of(speer(d) * 64, 64), 64)], dst_ref=rs.at[s],
            send_sem=sb_s.at[d], recv_sem=sb_r.at[d],
            device_id=(speer(d), t), device_id_type=MESH,
        )

    for d in order:
        sb_copy(d).start()
    rs[s] = so[pl.ds(pl.multiple_of(s * 64, 64), 64), :]

    for i, p in enumerate(peers):
        y_copy(p, y1, y_s.at[0], y_r.at[i]).wait_recv()
        c_copy(i + 1, p).start()
        if i > 0:
            @pl.when(inner)
            def _():
                y_copy(p, y1, f_s.at[i], y_r.at[i]).start()
        step(kvb.at[p, c], biasb[p, 0:1, :], False)
        c_arrival(i + 1, p).wait_recv()
        step(kvb.at[p, 1 - c], biasb[p, 0:1, :], False)

    for zz in range(8):
        rows = slice(zz * 64, zz * 64 + 64)
        ob[zz] = pack_part(mb[rows, :], accb[rows, :])

    def tb_copy(d):
        return pltpu.make_async_remote_copy(
            src_ref=ob.at[zpeer(d)], dst_ref=rt.at[z],
            send_sem=tb_s.at[d], recv_sem=tb_r.at[d],
            device_id=at(zpeer(d), y, c), device_id_type=MESH,
        )

    for d in order:
        tb_copy(d).start()
    rt[z] = ob[z]

    for d in order[::-1]:
        sb_copy(d).wait_recv()
    for d in order[::-1]:
        tb_copy(d).wait_recv()

    own = act_ref[0, z * 4 + y] > 0
    halves = []
    for h in range(8):
        a = rs[h].astype(F32)
        b = rt[h].astype(F32)
        la = unpack_lse(a)
        lb = jnp.where(own, unpack_lse(b), selfm[h, :, 0:1])
        b = jnp.where(own, b, sb[h, 0:64, :].astype(F32))
        m = jnp.maximum(la, lb)
        wa = jnp.exp2((la - m) * LOG2E)
        wb = jnp.exp2((lb - m) * LOG2E)
        inv = 1.0 / (wa + wb)
        halves.append(a * (wa * inv) + b * (wb * inv))
    pairs = [
        jnp.where(low, swap_halves(halves[2 * j]), halves[2 * j + 1]).astype(BF16) for j in range(4)
    ]
    attended = jnp.concatenate(pairs, axis=1)
    wcopy(3).wait()
    branch = jnp.dot(attended, wout[...], preferred_element_type=F32)
    out_ref[...] = (resid[...] + ada_ref[2:3, :] * branch).astype(BF16)

    for d in order:
        zk_copy(d).wait_send()
        zq_copy(d).wait_send()
        st_copy(d).wait_send()
        sb_copy(d).wait_send()
        tb_copy(d).wait_send()
    send_near.wait_send()
    send_far.wait_send()
    for i, p in enumerate((y,) + peers):
        c_copy(i, p).wait_send()

    @pl.when(inner)
    def _():
        for i in (1, 2):
            y_copy(peers[i], y1, f_s.at[i], y_r.at[i]).wait_send()


def body(hidden, control_ids, control_table, activity, ada, w_qkv, w_out):
    vmem = pl.BlockSpec(memory_space=pltpu.VMEM)
    anywhere = pl.BlockSpec(memory_space=pl.ANY)
    dma = pltpu.SemaphoreType.DMA
    out = pl.pallas_call(
        kernel,
        name="attention_block",
        out_shape=jax.ShapeDtypeStruct((FR, 1024), BF16),
        in_specs=[vmem, vmem, vmem, pl.BlockSpec(memory_space=pltpu.SMEM), vmem, anywhere, anywhere],
        out_specs=vmem,
        scratch_shapes=[
            pltpu.VMEM((3, 1024, 512), BF16),
            pltpu.VMEM((512, 1024), BF16),
            pltpu.VMEM((FR, 1024), F32),
            pltpu.VMEM((8, 96, LANES), BF16),
            pltpu.VMEM((4, 2, 512, LANES), BF16),
            pltpu.VMEM((8, 32, LANES), BF16),
            pltpu.VMEM((512, LANES), BF16),
            pltpu.VMEM((8, 96, LANES), BF16),
            pltpu.VMEM((512, LANES), BF16),
            pltpu.VMEM((512, LANES), F32),
            pltpu.VMEM((512, LANES), F32),
            pltpu.VMEM((4, 8, 512), F32),
            pltpu.VMEM((8, FR, LANES), F32),
            pltpu.VMEM((8, FR, LANES), BF16),
            pltpu.VMEM((512, LANES), BF16),
            pltpu.VMEM((8, FR, LANES), BF16),
            pltpu.VMEM((8, FR, LANES), BF16),
            dma((4,)),
            dma((8,)), dma((8,)), dma((8,)), dma((8,)), dma((8,)), dma((8,)),
            dma((2,)), dma((3,)), dma((3,)), dma((4,)), dma((4,)),
            dma((8,)), dma((8,)), dma((8,)), dma((8,)),
        ],
        compiler_params=pltpu.CompilerParams(
            collective_id=0, has_side_effects=True, vmem_limit_bytes=40 * 1024 * 1024
        ),
    )(hidden[0], control_ids[None, :], control_table, activity, ada[0], w_qkv, w_out)
    return out[None]


def solution(mesh):
    placed = (P("stem", "tm", None), P("tm"), P(), P("stem", None), P("stem", None, None), P(), P())
    return jax.shard_map(
        body, mesh=mesh, in_specs=placed, out_specs=P("stem", "tm", None), check_vma=False
    )
```

```python
import functools
import math

import jax
import jax.numpy as jnp
from jax import lax
from jax.experimental import pallas as pl
from jax.experimental.pallas import tpu as pltpu
from jax.sharding import PartitionSpec as P

MESH = pl.DeviceIdType.MESH
F32 = jnp.float32
BF16 = jnp.bfloat16
LOG2E = math.log2(math.e)
NEG = -1e30
FR = 64
LANES = 128
HALF = 256


def lane_iota(rows):
    return lax.broadcasted_iota(jnp.int32, (rows, LANES), 1)


def swap_halves(x):
    return pltpu.roll(x, 64, 1)


def nt_dot(a, b):
    return lax.dot_general(a, b, (((1,), (1,)), ((), ())), preferred_element_type=F32)


def unfold_low(f):
    return jnp.where(lane_iota(f.shape[0]) < 64, f, 0.0).astype(BF16)


def unfold_high(f):
    return unfold_low(swap_halves(f))


def ones_values(kv):
    return jnp.where(lane_iota(kv.shape[0]) < 64, jnp.ones_like(kv), kv)


def pack_part(m, acc):
    rows = acc.shape[0]
    lane = lane_iota(rows)
    total = jnp.where(lane < 64, acc, swap_halves(acc))
    value = acc / total
    lse = m + jnp.log(total)
    hi = lse.astype(BF16).astype(F32)
    mid = (lse - hi).astype(BF16).astype(F32)
    lo = lse - hi - mid
    return jnp.where(
        lane < 16, hi, jnp.where(lane < 32, mid, jnp.where(lane < 64, lo, value))
    ).astype(BF16)


def unpack_lse(part):
    return part[:, 0:1] + part[:, 16:17] + part[:, 32:33]


def kernel(
    hidden_ref, ids_ref, table_ref, act_ref, ada_ref, wqkv_hbm, wout_hbm, out_ref,
    wqkv, wout, resid, sb, kvb, qb, zb, rst, scb, mb, accb, biasb, selfm, ob, so, rt, rs,
    w_sem, zk_s, zk_r, zq_s, zq_r, st_s, st_r, y_s, y_r, f_s, c_s, c_r, tb_s, tb_r, sb_s, sb_r,
):
    s = lax.axis_index("stem")
    t = lax.axis_index("tm")
    z = lax.div(t, 8)
    y = lax.rem(lax.div(t, 2), 4)
    c = lax.rem(t, 2)
    y1 = y + 1 - 2 * lax.rem(y, 2)
    inner = jnp.logical_or(y == 1, y == 2)
    innerx = jnp.where(inner, 1, 0)
    p2 = jnp.where(inner, 3 - y, 3 - y1)
    p3 = jnp.where(inner, 3 - y1, 3 - y)
    peers = (y1, p2, p3)

    def at(zz, yy, cc):
        return (s, (zz * 4 + yy) * 2 + cc)

    def zpeer(d):
        return lax.rem(z + d, 8)

    def speer(d):
        return lax.rem(s + d, 8)

    core = at(z, y, 1 - c)

    barrier = pltpu.get_barrier_semaphore()
    for d in range(1, 8):
        pl.semaphore_signal(barrier, inc=1, device_id=at(zpeer(d), y, c), device_id_type=MESH)
        pl.semaphore_signal(barrier, inc=1, device_id=(speer(d), t), device_id_type=MESH)
    for p in peers:
        pl.semaphore_signal(barrier, inc=1, device_id=at(z, p, c), device_id_type=MESH)
    pl.semaphore_signal(barrier, inc=1, device_id=core, device_id_type=MESH)

    def wcopy(i):
        if i == 3:
            return pltpu.make_async_copy(wout_hbm, wout, w_sem.at[3])
        cols = pl.ds(i * 512, 512)
        return pltpu.make_async_copy(wqkv_hbm.at[:, cols], wqkv.at[i], w_sem.at[i])

    for i in (1, 2, 0, 3):
        wcopy(i).start()

    def ada_row(i):
        return jnp.concatenate([ada_ref[8 * i + k : 8 * i + k + 1, :] for k in range(8)], axis=1)

    onehot = (lax.broadcasted_iota(jnp.int32, (128, FR), 0) == ids_ref[...]).astype(BF16)
    lookup = lax.dot_general(
        onehot, table_ref[...], (((0,), (0,)), ((), ())), preferred_element_type=F32
    )
    residual = hidden_ref[...].astype(F32) + lookup
    resid[...] = residual
    mean = jnp.mean(residual, axis=-1, keepdims=True)
    cent = residual - mean
    var = jnp.mean(jnp.square(cent), axis=-1, keepdims=True)
    normed = (cent * lax.rsqrt(var + 1e-6) * (1.0 + ada_row(1)) + ada_row(0)).astype(BF16)

    low = lane_iota(FR) < 64
    wcopy(1).wait()
    keys = jnp.dot(normed, wqkv[1], preferred_element_type=F32)
    wcopy(2).wait()
    values = jnp.dot(normed, wqkv[2], preferred_element_type=F32)
    for j in range(4):
        k2 = keys[:, 128 * j : 128 * j + 128]
        v2 = values[:, 128 * j : 128 * j + 128]
        sb[2 * j, 0:64, :] = jnp.where(low, k2, swap_halves(v2)).astype(BF16)
        sb[2 * j + 1, 0:64, :] = jnp.where(low, swap_halves(k2), v2).astype(BF16)

    pl.semaphore_wait(barrier, 18)

    def zk_copy(d):
        return pltpu.make_async_remote_copy(
            src_ref=sb.at[zpeer(d), pl.ds(0, 64)],
            dst_ref=kvb.at[y, c, pl.ds(pl.multiple_of(z * 64, 64), 64)],
            send_sem=zk_s.at[d], recv_sem=zk_r.at[z],
            device_id=at(zpeer(d), y, c), device_id_type=MESH,
        )

    def zq_copy(d):
        return pltpu.make_async_remote_copy(
            src_ref=sb.at[zpeer(d), pl.ds(64, 32)],
            dst_ref=qb.at[z],
            send_sem=zq_s.at[d], recv_sem=zq_r.at[z],
            device_id=at(zpeer(d), y, c), device_id_type=MESH,
        )

    def st_copy(d):
        return pltpu.make_async_remote_copy(
            src_ref=sb.at[speer(d)], dst_ref=rst.at[s],
            send_sem=st_s.at[d], recv_sem=st_r.at[d],
            device_id=(speer(d), t), device_id_type=MESH,
        )

    order = (4, 3, 5, 2, 6, 1, 7)
    for d in order:
        zk_copy(d).start()

    wcopy(0).wait()
    queries = jnp.dot(normed, wqkv[0], preferred_element_type=F32).astype(BF16).astype(F32) * 0.125
    low32 = lane_iota(32) < 64
    for j in range(4):
        q2 = queries[:, 128 * j : 128 * j + 128]
        a, b = q2[0:32], q2[32:64]
        sb[2 * j, 64:96, :] = jnp.where(low32, a, swap_halves(b)).astype(BF16)
        sb[2 * j + 1, 64:96, :] = jnp.where(low32, swap_halves(a), b).astype(BF16)
    for d in order:
        zq_copy(d).start()
    for d in order:
        st_copy(d).start()

    own_kv = pltpu.make_async_copy(
        sb.at[z, pl.ds(0, 64)], kvb.at[y, c, pl.ds(pl.multiple_of(z * 64, 64), 64)], zk_r.at[z]
    )
    own_kv.start()
    own_q = pltpu.make_async_copy(sb.at[z, pl.ds(64, 32)], qb.at[z], zq_r.at[z])
    own_q.start()
    rst[s] = sb[s]
    group = lax.div(lax.broadcasted_iota(jnp.int32, (8, 512), 1), 64)
    for yy in range(4):
        row = jnp.zeros((8, 512), F32)
        for zz in range(8):
            bias = jnp.where(act_ref[0, zz * 4 + yy] > 0, 0.0, NEG).astype(F32)
            row = jnp.where(group == zz, bias, row)
        biasb[yy] = row
    for j in range(4):
        q2 = queries[:, 128 * j : 128 * j + 128]
        k2 = keys[:, 128 * j : 128 * j + 128].astype(BF16).astype(F32)
        prod = q2 * k2
        even = jnp.sum(jnp.where(low, prod, 0.0), axis=1, keepdims=True)
        odd = jnp.sum(jnp.where(low, 0.0, prod), axis=1, keepdims=True)
        selfm[2 * j] = jnp.broadcast_to(even, (FR, LANES))
        selfm[2 * j + 1] = jnp.broadcast_to(odd, (FR, LANES))

    def zk_wait(zz):
        block = kvb.at[y, c, pl.ds(zz * 64, 64)]
        pltpu.make_async_copy(block, block, zk_r.at[zz]).wait()

    def zq_wait(zz):
        pltpu.make_async_copy(qb.at[zz], qb.at[zz], zq_r.at[zz]).wait()

    def part(yy, cc, g):
        return kvb.at[yy, cc, pl.ds(g * HALF, HALF)]

    def c_copy(i, yy, g):
        return pltpu.make_async_remote_copy(
            src_ref=part(yy, c, g), dst_ref=part(yy, c, g),
            send_sem=c_s.at[4 * g + i], recv_sem=c_r.at[4 * g + i], device_id=core, device_id_type=MESH,
        )

    def c_arrival(i, yy, g):
        return pltpu.make_async_remote_copy(
            src_ref=part(yy, 1 - c, g), dst_ref=part(yy, 1 - c, g),
            send_sem=c_s.at[4 * g + i], recv_sem=c_r.at[4 * g + i], device_id=core, device_id_type=MESH,
        )

    def y_copy(block, target, ssem, rsem, g):
        return pltpu.make_async_remote_copy(
            src_ref=part(block, c, g), dst_ref=part(block, c, g),
            send_sem=ssem, recv_sem=rsem, device_id=at(z, target, c), device_id_type=MESH,
        )

    def send_near(g):
        return y_copy(y, y1, y_s.at[2 * g], y_r.at[3 * g], g)

    def send_far(g):
        return y_copy(y, p2, y_s.at[2 * g + 1], y_r.at[3 * g + 2 - innerx], g)

    def onward(i, g):
        return y_copy(peers[i], y1, f_s.at[2 * g + i - 1], y_r.at[3 * g + i], g)

    def gather_z(g):
        for zz in range(4 * g, 4 * g + 4):
            zk_wait(zz)
        send_far(g).start()
        send_near(g).start()
        c_copy(0, y, g).start()

    def gather_y(g):
        for i, p in enumerate(peers):
            y_copy(p, y1, y_s.at[2 * g], y_r.at[3 * g + i], g).wait_recv()
            if i > 0:
                @pl.when(inner)
                def _():
                    onward(i, g).start()
            c_copy(i + 1, p, g).start()

    def gather_core(g):
        for i, p in enumerate((y,) + peers):
            c_arrival(i, p, g).wait_recv()

    def take_queries(g):
        for zz in range(4 * g, 4 * g + 4):
            zq_wait(zz)
            f = qb[zz].astype(F32)
            zb[zz * 64 : zz * 64 + 32, :] = unfold_low(f)
            zb[zz * 64 + 32 : zz * 64 + 64, :] = unfold_high(f)

    def cell(g, kg):
        rows = slice(g * HALF, g * HALF + HALF)
        keys_at = [(yy, cc) for yy in range(4) for cc in range(2)]
        zq = zb[rows, :]
        top = None
        for b, (yy, cc) in enumerate(keys_at):
            kv = kvb[yy, cc, kg * HALF : kg * HALF + HALF, :]
            sc = nt_dot(zq, kv) + biasb[yy, 0:1, kg * HALF : kg * HALF + HALF]
            scb[kg, :, b * HALF : b * HALF + HALF] = sc
            for k in range(0, HALF, LANES):
                one = sc[:, k : k + LANES]
                top = one if top is None else jnp.maximum(top, one)
        m = jnp.broadcast_to(jnp.max(top, axis=1, keepdims=True), (HALF, LANES))
        if kg > 0:
            old = mb[rows, :]
            m = jnp.maximum(old, m)
        total = None
        for b, (yy, cc) in enumerate(keys_at):
            kv = kvb[yy, cc, kg * HALF : kg * HALF + HALF, :]
            p = jnp.exp2((scb[kg, :, b * HALF : b * HALF + HALF] - m[:, 0:1]) * LOG2E).astype(BF16)
            new = jnp.dot(p, ones_values(kv), preferred_element_type=F32)
            total = new if total is None else total + new
        if kg > 0:
            total = accb[rows, :] * jnp.exp2((old - m) * LOG2E) + total
        else:
            accb[rows, :] = total
            mb[rows, :] = m
        return m, total

    def tb_copy(zz):
        return pltpu.make_async_remote_copy(
            src_ref=ob.at[zz], dst_ref=rt.at[z],
            send_sem=tb_s.at[zz], recv_sem=tb_r.at[z],
            device_id=at(zz, y, c), device_id_type=MESH,
        )

    def give_back(g, m, total):
        packed = pack_part(m, total)
        for k in range(4):
            zz = 4 * g + k
            ob[zz] = packed[64 * k : 64 * k + 64, :]

            @pl.when(z != zz)
            def _():
                tb_copy(zz).start()

            @pl.when(z == zz)
            def _():
                pltpu.make_async_copy(ob.at[zz], rt.at[zz], tb_r.at[zz]).start()

    gather_z(0)
    take_queries(0)
    gather_z(1)
    gather_y(0)
    take_queries(1)
    gather_core(0)
    cell(0, 0)
    gather_y(1)

    for d in order[::-1]:
        st_copy(d).wait_recv()
    row = lax.broadcasted_iota(jnp.int32, (LANES, LANES), 0)
    col = lax.broadcasted_iota(jnp.int32, (LANES, LANES), 1)
    keep = jnp.logical_and(jnp.bitwise_and(row, 15) == jnp.bitwise_and(col, 15), row != col)
    for f0 in range(0, FR, 16):
        q0 = 64 + f0 % 32
        folded = jnp.concatenate([rst[ss, q0 : q0 + 16, :] for ss in range(8)], axis=0).astype(F32)
        qst = unfold_low(folded) if f0 < 32 else unfold_high(folded)
        kvst = jnp.concatenate([rst[ss, f0 : f0 + 16, :] for ss in range(8)], axis=0)
        sc = jnp.where(keep, nt_dot(qst, kvst), NEG)
        top = jnp.max(sc, axis=1, keepdims=True)
        p = jnp.exp2((sc - top) * LOG2E).astype(BF16)
        done = pack_part(top, jnp.dot(p, ones_values(kvst), preferred_element_type=F32))
        for ss in range(8):
            so[ss, f0 : f0 + 16, :] = done[16 * ss : 16 * ss + 16, :]

    def sb_copy(d):
        return pltpu.make_async_remote_copy(
            src_ref=so.at[speer(d)], dst_ref=rs.at[s],
            send_sem=sb_s.at[d], recv_sem=sb_r.at[d],
            device_id=(speer(d), t), device_id_type=MESH,
        )

    for d in order:
        sb_copy(d).start()
    rs[s] = so[s]

    gather_core(1)
    give_back(0, *cell(0, 1))
    cell(1, 0)
    give_back(1, *cell(1, 1))

    for d in order[::-1]:
        sb_copy(d).wait_recv()
    for zz in range(8):
        pltpu.make_async_copy(rt.at[zz], rt.at[zz], tb_r.at[zz]).wait()

    own = act_ref[0, z * 4 + y] > 0
    halves = []
    for h in range(8):
        a = rs[h].astype(F32)
        b = rt[h].astype(F32)
        la = unpack_lse(a)
        lb = jnp.where(own, unpack_lse(b), selfm[h, :, 0:1])
        b = jnp.where(own, b, sb[h, 0:64, :].astype(F32))
        m = jnp.maximum(la, lb)
        wa = jnp.exp2((la - m) * LOG2E)
        wb = jnp.exp2((lb - m) * LOG2E)
        inv = 1.0 / (wa + wb)
        halves.append(a * (wa * inv) + b * (wb * inv))
    pairs = [
        jnp.where(low, swap_halves(halves[2 * j]), halves[2 * j + 1]).astype(BF16) for j in range(4)
    ]
    attended = jnp.concatenate(pairs, axis=1)
    wcopy(3).wait()
    branch = jnp.dot(attended, wout[...], preferred_element_type=F32)
    out_ref[...] = (resid[...] + ada_row(2) * branch).astype(BF16)

    for d in order:
        zk_copy(d).wait_send()
        zq_copy(d).wait_send()
        st_copy(d).wait_send()
        sb_copy(d).wait_send()
    for zz in range(8):
        @pl.when(z != zz)
        def _():
            tb_copy(zz).wait_send()
    for g in range(2):
        send_near(g).wait_send()
        send_far(g).wait_send()
        for i, p in enumerate((y,) + peers):
            c_copy(i, p, g).wait_send()

        @pl.when(inner)
        def _():
            for i in (1, 2):
                onward(i, g).wait_send()


def body(hidden, control_ids, control_table, activity, ada, w_qkv, w_out):
    vmem = pl.BlockSpec(memory_space=pltpu.VMEM)
    anywhere = pl.BlockSpec(memory_space=pl.ANY)
    dma = pltpu.SemaphoreType.DMA
    out = pl.pallas_call(
        kernel,
        name="attention_block",
        out_shape=jax.ShapeDtypeStruct((FR, 1024), BF16),
        in_specs=[vmem, vmem, vmem, pl.BlockSpec(memory_space=pltpu.SMEM), vmem, anywhere, anywhere],
        out_specs=vmem,
        scratch_shapes=[
            pltpu.VMEM((3, 1024, 512), BF16),
            pltpu.VMEM((512, 1024), BF16),
            pltpu.VMEM((FR, 1024), F32),
            pltpu.VMEM((8, 96, LANES), BF16),
            pltpu.VMEM((4, 2, 512, LANES), BF16),
            pltpu.VMEM((8, 32, LANES), BF16),
            pltpu.VMEM((512, LANES), BF16),
            pltpu.VMEM((8, 96, LANES), BF16),
            pltpu.VMEM((2, HALF, 8 * HALF), F32),
            pltpu.VMEM((512, LANES), F32),
            pltpu.VMEM((512, LANES), F32),
            pltpu.VMEM((4, 8, 512), F32),
            pltpu.VMEM((8, FR, LANES), F32),
            pltpu.VMEM((8, FR, LANES), BF16),
            pltpu.VMEM((8, FR, LANES), BF16),
            pltpu.VMEM((8, FR, LANES), BF16),
            pltpu.VMEM((8, FR, LANES), BF16),
            dma((4,)),
            dma((8,)), dma((8,)), dma((8,)), dma((8,)), dma((8,)), dma((8,)),
            dma((4,)), dma((6,)), dma((4,)), dma((8,)), dma((8,)),
            dma((8,)), dma((8,)), dma((8,)), dma((8,)),
        ],
        compiler_params=pltpu.CompilerParams(
            collective_id=0, has_side_effects=True, vmem_limit_bytes=60 * 1024 * 1024
        ),
    )(hidden[0], control_ids[None, :], control_table, activity, ada.reshape(24, LANES), w_qkv, w_out)
    return out[None]


def solution(mesh):
    placed = (P("stem", "tm", None), P("tm"), P(), P("stem", None), P("stem", None, None), P(), P())
    return jax.shard_map(
        body, mesh=mesh, in_specs=placed, out_specs=P("stem", "tm", None), check_vma=False
    )
```

```python
import functools
import math

import jax
import jax.numpy as jnp
from jax import lax
from jax.experimental import pallas as pl
from jax.experimental.pallas import tpu as pltpu
from jax.sharding import PartitionSpec as P

MESH = pl.DeviceIdType.MESH
F32 = jnp.float32
BF16 = jnp.bfloat16
LOG2E = math.log2(math.e)
NEG = -1e30
FR = 64
LANES = 128
HALF = 256


def lane_iota(rows):
    return lax.broadcasted_iota(jnp.int32, (rows, LANES), 1)


def swap_halves(x):
    return pltpu.roll(x, 64, 1)


def nt_dot(a, b):
    return lax.dot_general(a, b, (((1,), (1,)), ((), ())), preferred_element_type=F32)


def unfold_low(f):
    return jnp.where(lane_iota(f.shape[0]) < 64, f, 0.0).astype(BF16)


def unfold_high(f):
    return unfold_low(swap_halves(f))


def ones_values(kv):
    return jnp.where(lane_iota(kv.shape[0]) < 64, jnp.ones_like(kv), kv)


def pack_part(m, acc):
    rows = acc.shape[0]
    lane = lane_iota(rows)
    total = jnp.where(lane < 64, acc, swap_halves(acc))
    value = acc / total
    lse = m + jnp.log(total)
    hi = lse.astype(BF16).astype(F32)
    mid = (lse - hi).astype(BF16).astype(F32)
    lo = lse - hi - mid
    return jnp.where(
        lane < 16, hi, jnp.where(lane < 32, mid, jnp.where(lane < 64, lo, value))
    ).astype(BF16)


def unpack_lse(part):
    return part[:, 0:1] + part[:, 16:17] + part[:, 32:33]


def kernel(
    hidden_hbm, ids_hbm, table_hbm, act_hbm, ada_hbm, wqkv_hbm, wout_hbm, out_ref,
    hidden_ref, ids_ref, table_ref, act_ref, ada_ref,
    wqkv, wout, resid, sb, kvb, qb, qo, zb, zo, rst, scb, mb, accb, biasb, selfm, ob, oo, so, rt, ro, rs,
    i_sem, w_sem, zk_s, zk_r, zq_s, zq_r, st_s, st_r, y_s, y_r, f_s, c_s, c_r, o_s, o_r, u_s, u_r, tb_s, tb_r, sb_s, sb_r,
):
    s = lax.axis_index("stem")
    t = lax.axis_index("tm")
    z = lax.div(t, 8)
    y = lax.rem(lax.div(t, 2), 4)
    c = lax.rem(t, 2)
    y1 = y + 1 - 2 * lax.rem(y, 2)
    inner = jnp.logical_or(y == 1, y == 2)
    outer = jnp.logical_not(inner)
    far_inner = 3 - y
    pair = lax.div(y, 2)

    def at(zz, yy, cc):
        return (s, (zz * 4 + yy) * 2 + cc)

    def zpeer(d):
        return lax.rem(z + d, 8)

    def speer(d):
        return lax.rem(s + d, 8)

    core = at(z, y, 1 - c)

    barrier = pltpu.get_barrier_semaphore()
    for d in range(1, 8):
        pl.semaphore_signal(barrier, inc=1, device_id=at(zpeer(d), y, c), device_id_type=MESH)
        pl.semaphore_signal(barrier, inc=1, device_id=(speer(d), t), device_id_type=MESH)
    pl.semaphore_signal(barrier, inc=1, device_id=at(z, y1, c), device_id_type=MESH)

    @pl.when(inner)
    def _():
        pl.semaphore_signal(barrier, inc=1, device_id=at(z, far_inner, c), device_id_type=MESH)

    @pl.when(outer)
    def _():
        for d in range(1, 8):
            pl.semaphore_signal(barrier, inc=1, device_id=at(zpeer(d), y1, c), device_id_type=MESH)

    pl.semaphore_signal(barrier, inc=1, device_id=core, device_id_type=MESH)

    def wcopy(i):
        if i == 3:
            return pltpu.make_async_copy(wout_hbm, wout, w_sem.at[3])
        cols = pl.ds(i * 512, 512)
        return pltpu.make_async_copy(wqkv_hbm.at[:, cols], wqkv.at[i], w_sem.at[i])

    small = [
        pltpu.make_async_copy(src, dst, i_sem.at[n])
        for n, (src, dst) in enumerate(
            (
                (hidden_hbm, hidden_ref), (ids_hbm, ids_ref), (table_hbm, table_ref),
                (ada_hbm, ada_ref), (act_hbm, act_ref),
            )
        )
    ]
    for copy in small:
        copy.start()
    for i in (1, 2, 0, 3):
        wcopy(i).start()
    for copy in small:
        copy.wait()

    def ada_row(i):
        return jnp.concatenate([ada_ref[8 * i + k : 8 * i + k + 1, :] for k in range(8)], axis=1)

    onehot = (lax.broadcasted_iota(jnp.int32, (128, FR), 0) == ids_ref[...]).astype(BF16)
    lookup = lax.dot_general(
        onehot, table_ref[...], (((0,), (0,)), ((), ())), preferred_element_type=F32
    )
    residual = hidden_ref[...].astype(F32) + lookup
    resid[...] = residual
    mean = jnp.mean(residual, axis=-1, keepdims=True)
    cent = residual - mean
    var = jnp.mean(jnp.square(cent), axis=-1, keepdims=True)
    normed = (cent * lax.rsqrt(var + 1e-6) * (1.0 + ada_row(1)) + ada_row(0)).astype(BF16)

    low = lane_iota(FR) < 64
    wcopy(1).wait()
    keys = jnp.dot(normed, wqkv[1], preferred_element_type=F32)
    wcopy(2).wait()
    values = jnp.dot(normed, wqkv[2], preferred_element_type=F32)
    for j in range(4):
        k2 = keys[:, 128 * j : 128 * j + 128]
        v2 = values[:, 128 * j : 128 * j + 128]
        sb[2 * j, 0:64, :] = jnp.where(low, k2, swap_halves(v2)).astype(BF16)
        sb[2 * j + 1, 0:64, :] = jnp.where(low, swap_halves(k2), v2).astype(BF16)

    pl.semaphore_wait(barrier, jnp.where(inner, 24, 16))

    def zk_copy(d):
        return pltpu.make_async_remote_copy(
            src_ref=sb.at[zpeer(d), pl.ds(0, 64)],
            dst_ref=kvb.at[y, c, pl.ds(pl.multiple_of(z * 64, 64), 64)],
            send_sem=zk_s.at[d], recv_sem=zk_r.at[z],
            device_id=at(zpeer(d), y, c), device_id_type=MESH,
        )

    def zq_copy(d):
        return pltpu.make_async_remote_copy(
            src_ref=sb.at[zpeer(d), pl.ds(64, 32)],
            dst_ref=qb.at[z],
            send_sem=zq_s.at[d], recv_sem=zq_r.at[z],
            device_id=at(zpeer(d), y, c), device_id_type=MESH,
        )

    def st_copy(d):
        return pltpu.make_async_remote_copy(
            src_ref=sb.at[speer(d)], dst_ref=rst.at[s],
            send_sem=st_s.at[d], recv_sem=st_r.at[d],
            device_id=(speer(d), t), device_id_type=MESH,
        )

    order = (4, 3, 5, 2, 6, 1, 7)
    for d in order:
        zk_copy(d).start()

    wcopy(0).wait()
    queries = jnp.dot(normed, wqkv[0], preferred_element_type=F32).astype(BF16).astype(F32) * 0.125
    low32 = lane_iota(32) < 64
    for j in range(4):
        q2 = queries[:, 128 * j : 128 * j + 128]
        a, b = q2[0:32], q2[32:64]
        sb[2 * j, 64:96, :] = jnp.where(low32, a, swap_halves(b)).astype(BF16)
        sb[2 * j + 1, 64:96, :] = jnp.where(low32, swap_halves(a), b).astype(BF16)
    for d in order:
        zq_copy(d).start()
    for d in order:
        st_copy(d).start()

    own_kv = pltpu.make_async_copy(
        sb.at[z, pl.ds(0, 64)], kvb.at[y, c, pl.ds(pl.multiple_of(z * 64, 64), 64)], zk_r.at[z]
    )
    own_kv.start()
    own_q = pltpu.make_async_copy(sb.at[z, pl.ds(64, 32)], qb.at[z], zq_r.at[z])
    own_q.start()
    rst[s] = sb[s]
    group = lax.div(lax.broadcasted_iota(jnp.int32, (8, 512), 1), 64)
    for yy in range(4):
        row = jnp.zeros((8, 512), F32)
        for zz in range(8):
            bias = jnp.where(act_ref[0, zz * 4 + yy] > 0, 0.0, NEG).astype(F32)
            row = jnp.where(group == zz, bias, row)
        biasb[yy] = row
    for j in range(4):
        q2 = queries[:, 128 * j : 128 * j + 128]
        k2 = keys[:, 128 * j : 128 * j + 128].astype(BF16).astype(F32)
        prod = q2 * k2
        even = jnp.sum(jnp.where(low, prod, 0.0), axis=1, keepdims=True)
        odd = jnp.sum(jnp.where(low, 0.0, prod), axis=1, keepdims=True)
        selfm[2 * j] = jnp.broadcast_to(even, (FR, LANES))
        selfm[2 * j + 1] = jnp.broadcast_to(odd, (FR, LANES))

    def zk_wait(zz):
        block = kvb.at[y, c, pl.ds(zz * 64, 64)]
        pltpu.make_async_copy(block, block, zk_r.at[zz]).wait()

    def zq_wait(zz):
        pltpu.make_async_copy(qb.at[zz], qb.at[zz], zq_r.at[zz]).wait()

    def part(yy, cc, g):
        return kvb.at[yy, cc, pl.ds(g * HALF, HALF)]

    held = (y, y1, far_inner, jnp.where(inner, 3 - y1, 0))

    def c_copy(i, g):
        return pltpu.make_async_remote_copy(
            src_ref=part(held[i], c, g), dst_ref=part(held[i], c, g),
            send_sem=c_s.at[4 * g + i], recv_sem=c_r.at[4 * g + i], device_id=core, device_id_type=MESH,
        )

    def c_arrival(i, g):
        return pltpu.make_async_remote_copy(
            src_ref=part(held[i], 1 - c, g), dst_ref=part(held[i], 1 - c, g),
            send_sem=c_s.at[4 * g + i], recv_sem=c_r.at[4 * g + i], device_id=core, device_id_type=MESH,
        )

    def y_copy(block, target, ssem, rsem, g):
        return pltpu.make_async_remote_copy(
            src_ref=part(block, c, g), dst_ref=part(block, c, g),
            send_sem=ssem, recv_sem=rsem, device_id=at(z, target, c), device_id_type=MESH,
        )

    def send_near(g):
        return y_copy(y, y1, y_s.at[2 * g], y_r.at[3 * g], g)

    def send_far(g):
        return y_copy(y, far_inner, y_s.at[2 * g + 1], y_r.at[3 * g + 1], g)

    def onward(g):
        return y_copy(y1, far_inner, f_s.at[g], y_r.at[3 * g + 2], g)

    def lend_queries():
        return pltpu.make_async_remote_copy(
            src_ref=qb, dst_ref=qo, send_sem=o_s, recv_sem=o_r,
            device_id=at(z, y1, c), device_id_type=MESH,
        )

    def gather_z(g):
        for zz in range(4 * g, 4 * g + 4):
            zk_wait(zz)

        @pl.when(inner)
        def _():
            send_far(g).start()

        send_near(g).start()
        c_copy(0, g).start()

    def gather_near(g):
        y_copy(y1, y1, y_s.at[2 * g], y_r.at[3 * g], g).wait_recv()

        @pl.when(inner)
        def _():
            onward(g).start()

        c_copy(1, g).start()

    def gather_far(i, g):
        y_copy(held[i], far_inner, f_s.at[g], y_r.at[3 * g + i - 1], g).wait_recv()
        c_copy(i, g).start()

    def gather_core(i):
        for g in range(2):
            c_arrival(i, g).wait_recv()

    def unfold(source, target):
        for zz in range(8):
            f = source[zz].astype(F32)
            target[zz * 64 : zz * 64 + 32, :] = unfold_low(f)
            target[zz * 64 + 32 : zz * 64 + 64, :] = unfold_high(f)

    def cell(queries_ref, g, which, old=None):
        rows = slice(g * HALF, g * HALF + HALF)
        keys_at = [(2 * which + i, cc) for i in range(2) for cc in range(2)]
        zq = queries_ref[rows, :]
        top = None
        for b, (yy, cc) in enumerate(keys_at):
            sc = nt_dot(zq, kvb[yy, cc]) + biasb[yy, 0:1, :]
            scb[g, :, 512 * b : 512 * b + 512] = sc
            for k in range(0, 512, LANES):
                one = sc[:, k : k + LANES]
                top = one if top is None else jnp.maximum(top, one)
        m = jnp.broadcast_to(jnp.max(top, axis=1, keepdims=True), (HALF, LANES))
        if old is not None:
            m = jnp.maximum(old[0], m)
        total = None
        for b, (yy, cc) in enumerate(keys_at):
            p = jnp.exp2((scb[g, :, 512 * b : 512 * b + 512] - m[:, 0:1]) * LOG2E).astype(BF16)
            new = jnp.dot(p, ones_values(kvb[yy, cc]), preferred_element_type=F32)
            total = new if total is None else total + new
        if old is not None:
            total = old[1] * jnp.exp2((old[0] - m) * LOG2E) + total
        return m, total

    def kept(g):
        rows = slice(g * HALF, g * HALF + HALF)
        return mb[rows, :], accb[rows, :]

    def tb_copy(zz):
        return pltpu.make_async_remote_copy(
            src_ref=ob.at[zz], dst_ref=rt.at[z],
            send_sem=tb_s.at[zz], recv_sem=tb_r.at[z],
            device_id=at(zz, y, c), device_id_type=MESH,
        )

    def tu_copy(zz):
        return pltpu.make_async_remote_copy(
            src_ref=oo.at[zz], dst_ref=ro.at[z],
            send_sem=u_s.at[zz], recv_sem=u_r.at[z],
            device_id=at(zz, y1, c), device_id_type=MESH,
        )

    def give_lent(g, m, total):
        packed = pack_part(m, total)
        for k in range(4):
            zz = 4 * g + k
            oo[zz] = packed[64 * k : 64 * k + 64, :]
            tu_copy(zz).start()

    def give_back(g, m, total):
        packed = pack_part(m, total)
        for k in range(4):
            zz = 4 * g + k
            ob[zz] = packed[64 * k : 64 * k + 64, :]

            @pl.when(z != zz)
            def _():
                tb_copy(zz).start()

            @pl.when(z == zz)
            def _():
                pltpu.make_async_copy(ob.at[zz], rt.at[zz], tb_r.at[zz]).start()

    gather_z(0)
    gather_z(1)
    for zz in range(8):
        zq_wait(zz)

    @pl.when(outer)
    def _():
        lend_queries().start()

    unfold(qb, zb)
    for g in range(2):
        gather_near(g)

    @pl.when(inner)
    def _():
        for g in range(2):
            gather_far(2, g)
        lend_queries().wait_recv()
        unfold(qo, zo)

    gather_core(0)
    gather_core(1)
    for g in range(2):
        m, total = cell(zb, g, pair)
        mb[g * HALF : g * HALF + HALF, :] = m
        accb[g * HALF : g * HALF + HALF, :] = total

    @pl.when(outer)
    def _():
        for g in range(2):
            give_back(g, *kept(g))

    @pl.when(inner)
    def _():
        for g in range(2):
            gather_far(3, g)

    for d in order[::-1]:
        st_copy(d).wait_recv()
    row = lax.broadcasted_iota(jnp.int32, (LANES, LANES), 0)
    col = lax.broadcasted_iota(jnp.int32, (LANES, LANES), 1)
    keep = jnp.logical_and(jnp.bitwise_and(row, 15) == jnp.bitwise_and(col, 15), row != col)
    for f0 in range(0, FR, 16):
        q0 = 64 + f0 % 32
        folded = jnp.concatenate([rst[ss, q0 : q0 + 16, :] for ss in range(8)], axis=0).astype(F32)
        qst = unfold_low(folded) if f0 < 32 else unfold_high(folded)
        kvst = jnp.concatenate([rst[ss, f0 : f0 + 16, :] for ss in range(8)], axis=0)
        sc = jnp.where(keep, nt_dot(qst, kvst), NEG)
        top = jnp.max(sc, axis=1, keepdims=True)
        p = jnp.exp2((sc - top) * LOG2E).astype(BF16)
        done = pack_part(top, jnp.dot(p, ones_values(kvst), preferred_element_type=F32))
        for ss in range(8):
            so[ss, f0 : f0 + 16, :] = done[16 * ss : 16 * ss + 16, :]

    def sb_copy(d):
        return pltpu.make_async_remote_copy(
            src_ref=so.at[speer(d)], dst_ref=rs.at[s],
            send_sem=sb_s.at[d], recv_sem=sb_r.at[d],
            device_id=(speer(d), t), device_id_type=MESH,
        )

    for d in order:
        sb_copy(d).start()
    rs[s] = so[s]

    @pl.when(inner)
    def _():
        gather_core(2)
        gather_core(3)
        for g in range(2):
            give_lent(g, *cell(zo, g, 1 - pair))
        for g in range(2):
            give_back(g, *cell(zb, g, 1 - pair, kept(g)))

    for d in order[::-1]:
        sb_copy(d).wait_recv()
    for zz in range(8):
        pltpu.make_async_copy(rt.at[zz], rt.at[zz], tb_r.at[zz]).wait()

    @pl.when(outer)
    def _():
        for zz in range(8):
            pltpu.make_async_copy(ro.at[zz], ro.at[zz], u_r.at[zz]).wait()

    @pl.when(inner)
    def _():
        ro[...] = jnp.full((8, FR, LANES), NEG, BF16)

    own = act_ref[0, z * 4 + y] > 0
    halves = []
    for h in range(8):
        a = rs[h].astype(F32)
        b = rt[h].astype(F32)
        la = unpack_lse(a)
        lb = jnp.where(own, unpack_lse(b), selfm[h, :, 0:1])
        b = jnp.where(own, b, sb[h, 0:64, :].astype(F32))
        e = ro[h].astype(F32)
        le = jnp.where(own, unpack_lse(e), NEG)
        m = jnp.maximum(jnp.maximum(la, lb), le)
        wa = jnp.exp2((la - m) * LOG2E)
        wb = jnp.exp2((lb - m) * LOG2E)
        we = jnp.exp2((le - m) * LOG2E)
        inv = 1.0 / (wa + wb + we)
        halves.append(a * (wa * inv) + b * (wb * inv) + e * (we * inv))
    pairs = [
        jnp.where(low, swap_halves(halves[2 * j]), halves[2 * j + 1]).astype(BF16) for j in range(4)
    ]
    attended = jnp.concatenate(pairs, axis=1)
    wcopy(3).wait()
    branch = jnp.dot(attended, wout[...], preferred_element_type=F32)
    out_ref[...] = (resid[...] + ada_row(2) * branch).astype(BF16)

    for d in order:
        zk_copy(d).wait_send()
        zq_copy(d).wait_send()
        st_copy(d).wait_send()
        sb_copy(d).wait_send()
    for zz in range(8):
        @pl.when(z != zz)
        def _():
            tb_copy(zz).wait_send()
    for g in range(2):
        send_near(g).wait_send()
        c_copy(0, g).wait_send()
        c_copy(1, g).wait_send()

    @pl.when(outer)
    def _():
        lend_queries().wait_send()

    @pl.when(inner)
    def _():
        for g in range(2):
            send_far(g).wait_send()
            onward(g).wait_send()
            c_copy(2, g).wait_send()
            c_copy(3, g).wait_send()
        for zz in range(8):
            tu_copy(zz).wait_send()


def body(hidden, control_ids, control_table, activity, ada, w_qkv, w_out):
    vmem = pl.BlockSpec(memory_space=pltpu.VMEM)
    anywhere = pl.BlockSpec(memory_space=pl.ANY)
    dma = pltpu.SemaphoreType.DMA
    out = pl.pallas_call(
        kernel,
        name="attention_block",
        out_shape=jax.ShapeDtypeStruct((FR, 1024), BF16),
        in_specs=[anywhere] * 7,
        out_specs=vmem,
        scratch_shapes=[
            pltpu.VMEM((FR, 1024), BF16),
            pltpu.VMEM((1, FR), jnp.int32),
            pltpu.VMEM((128, 1024), BF16),
            pltpu.SMEM((1, 32), jnp.int32),
            pltpu.VMEM((24, LANES), F32),
            pltpu.VMEM((3, 1024, 512), BF16),
            pltpu.VMEM((512, 1024), BF16),
            pltpu.VMEM((FR, 1024), F32),
            pltpu.VMEM((8, 96, LANES), BF16),
            pltpu.VMEM((4, 2, 512, LANES), BF16),
            pltpu.VMEM((8, 32, LANES), BF16),
            pltpu.VMEM((8, 32, LANES), BF16),
            pltpu.VMEM((512, LANES), BF16),
            pltpu.VMEM((512, LANES), BF16),
            pltpu.VMEM((8, 96, LANES), BF16),
            pltpu.VMEM((2, HALF, 8 * HALF), F32),
            pltpu.VMEM((512, LANES), F32),
            pltpu.VMEM((512, LANES), F32),
            pltpu.VMEM((4, 8, 512), F32),
            pltpu.VMEM((8, FR, LANES), F32),
            pltpu.VMEM((8, FR, LANES), BF16),
            pltpu.VMEM((8, FR, LANES), BF16),
            pltpu.VMEM((8, FR, LANES), BF16),
            pltpu.VMEM((8, FR, LANES), BF16),
            pltpu.VMEM((8, FR, LANES), BF16),
            pltpu.VMEM((8, FR, LANES), BF16),
            dma((5,)),
            dma((4,)),
            dma((8,)), dma((8,)), dma((8,)), dma((8,)), dma((8,)), dma((8,)),
            dma((4,)), dma((6,)), dma((2,)), dma((8,)), dma((8,)), dma, dma, dma((8,)), dma((8,)),
            dma((8,)), dma((8,)), dma((8,)), dma((8,)),
        ],
        compiler_params=pltpu.CompilerParams(
            collective_id=0, has_side_effects=True, vmem_limit_bytes=60 * 1024 * 1024
        ),
    )(hidden[0], control_ids[None, :], control_table, activity, ada.reshape(24, LANES), w_qkv, w_out)
    return out[None]


def solution(mesh):
    placed = (P("stem", "tm", None), P("tm"), P(), P("stem", None), P("stem", None, None), P(), P())
    return jax.shard_map(
        body, mesh=mesh, in_specs=placed, out_specs=P("stem", "tm", None), check_vma=False
    )
```

```python
import functools
import math

import jax
import jax.numpy as jnp
from jax import lax
from jax.experimental import pallas as pl
from jax.experimental.pallas import tpu as pltpu
from jax.sharding import PartitionSpec as P

MESH = pl.DeviceIdType.MESH
F32 = jnp.float32
BF16 = jnp.bfloat16
LOG2E = math.log2(math.e)
NEG = -1e30
FR = 64
LANES = 128
HALF = 256


def lane_iota(rows):
    return lax.broadcasted_iota(jnp.int32, (rows, LANES), 1)


def swap_halves(x):
    return pltpu.roll(x, 64, 1)


def nt_dot(a, b):
    return lax.dot_general(a, b, (((1,), (1,)), ((), ())), preferred_element_type=F32)


def unfold_low(f):
    return jnp.where(lane_iota(f.shape[0]) < 64, f, 0.0).astype(BF16)


def unfold_high(f):
    return unfold_low(swap_halves(f))


def ones_values(kv):
    return jnp.where(lane_iota(kv.shape[0]) < 64, jnp.ones_like(kv), kv)


def pack_part(m, acc):
    rows = acc.shape[0]
    lane = lane_iota(rows)
    total = jnp.where(lane < 64, acc, swap_halves(acc))
    value = acc / total
    lse = m + jnp.log(total)
    hi = lse.astype(BF16).astype(F32)
    mid = (lse - hi).astype(BF16).astype(F32)
    lo = lse - hi - mid
    return jnp.where(
        lane < 16, hi, jnp.where(lane < 32, mid, jnp.where(lane < 64, lo, value))
    ).astype(BF16)


def unpack_lse(part):
    return part[:, 0:1] + part[:, 16:17] + part[:, 32:33]


def kernel(
    hidden_hbm, ids_hbm, table_hbm, act_hbm, ada_hbm, wqkv_hbm, wout_hbm, out_ref,
    hidden_ref, ids_ref, table_ref, act_ref, ada_ref,
    wqkv, wout, resid, sb, kvb, qb, qo, zb, zo, rst, scb, mb, accb, biasb, selfm, ob, oo, so, rt, ro, rs,
    i_sem, w_sem, zk_s, zk_r, zq_s, zq_r, st_s, st_r, y_s, y_r, f_s, c_s, c_r, o_s, o_r, u_s, u_r, tb_s, tb_r, sb_s, sb_r,
):
    s = lax.axis_index("stem")
    t = lax.axis_index("tm")
    z = lax.div(t, 8)
    y = lax.rem(lax.div(t, 2), 4)
    c = lax.rem(t, 2)
    y1 = y + 1 - 2 * lax.rem(y, 2)
    inner = jnp.logical_or(y == 1, y == 2)
    outer = jnp.logical_not(inner)
    far_inner = 3 - y
    pair = lax.div(y, 2)

    def at(zz, yy, cc):
        return (s, (zz * 4 + yy) * 2 + cc)

    def zpeer(d):
        return lax.rem(z + d, 8)

    def speer(d):
        return lax.rem(s + d, 8)

    core = at(z, y, 1 - c)

    barrier = pltpu.get_barrier_semaphore()
    for d in range(1, 8):
        pl.semaphore_signal(barrier, inc=1, device_id=at(zpeer(d), y, c), device_id_type=MESH)
        pl.semaphore_signal(barrier, inc=1, device_id=(speer(d), t), device_id_type=MESH)
    pl.semaphore_signal(barrier, inc=1, device_id=at(z, y1, c), device_id_type=MESH)

    @pl.when(inner)
    def _():
        pl.semaphore_signal(barrier, inc=1, device_id=at(z, far_inner, c), device_id_type=MESH)

    @pl.when(outer)
    def _():
        for d in range(1, 8):
            pl.semaphore_signal(barrier, inc=1, device_id=at(zpeer(d), y1, c), device_id_type=MESH)

    pl.semaphore_signal(barrier, inc=1, device_id=core, device_id_type=MESH)

    def wcopy(i):
        if i == 3:
            return pltpu.make_async_copy(wout_hbm, wout, w_sem.at[3])
        cols = pl.ds(i * 512, 512)
        return pltpu.make_async_copy(wqkv_hbm.at[:, cols], wqkv.at[i], w_sem.at[i])

    small = [
        pltpu.make_async_copy(src, dst, i_sem.at[n])
        for n, (src, dst) in enumerate(
            (
                (hidden_hbm, hidden_ref), (ids_hbm, ids_ref), (table_hbm, table_ref),
                (ada_hbm, ada_ref), (act_hbm, act_ref),
            )
        )
    ]
    for copy in small:
        copy.start()
    for i in (1, 2, 0, 3):
        wcopy(i).start()
    for copy in small:
        copy.wait()

    def ada_row(i):
        return jnp.concatenate([ada_ref[8 * i + k : 8 * i + k + 1, :] for k in range(8)], axis=1)

    onehot = (lax.broadcasted_iota(jnp.int32, (128, FR), 0) == ids_ref[...]).astype(BF16)
    lookup = lax.dot_general(
        onehot, table_ref[...], (((0,), (0,)), ((), ())), preferred_element_type=F32
    )
    residual = hidden_ref[...].astype(F32) + lookup
    resid[...] = residual
    mean = jnp.mean(residual, axis=-1, keepdims=True)
    cent = residual - mean
    var = jnp.mean(jnp.square(cent), axis=-1, keepdims=True)
    normed = (cent * lax.rsqrt(var + 1e-6) * (1.0 + ada_row(1)) + ada_row(0)).astype(BF16)

    low = lane_iota(FR) < 64
    wcopy(1).wait()
    keys = jnp.dot(normed, wqkv[1], preferred_element_type=F32)
    wcopy(2).wait()
    values = jnp.dot(normed, wqkv[2], preferred_element_type=F32)
    for j in range(4):
        k2 = keys[:, 128 * j : 128 * j + 128]
        v2 = values[:, 128 * j : 128 * j + 128]
        sb[2 * j, 0:64, :] = jnp.where(low, k2, swap_halves(v2)).astype(BF16)
        sb[2 * j + 1, 0:64, :] = jnp.where(low, swap_halves(k2), v2).astype(BF16)

    pl.semaphore_wait(barrier, jnp.where(inner, 24, 16))

    def zk_copy(d):
        return pltpu.make_async_remote_copy(
            src_ref=sb.at[zpeer(d), pl.ds(0, 64)],
            dst_ref=kvb.at[y, c, pl.ds(pl.multiple_of(z * 64, 64), 64)],
            send_sem=zk_s.at[d], recv_sem=zk_r.at[z],
            device_id=at(zpeer(d), y, c), device_id_type=MESH,
        )

    def zq_copy(d):
        return pltpu.make_async_remote_copy(
            src_ref=sb.at[zpeer(d), pl.ds(64, 32)],
            dst_ref=qb.at[z],
            send_sem=zq_s.at[d], recv_sem=zq_r.at[z],
            device_id=at(zpeer(d), y, c), device_id_type=MESH,
        )

    def st_copy(d):
        return pltpu.make_async_remote_copy(
            src_ref=sb.at[speer(d)], dst_ref=rst.at[s],
            send_sem=st_s.at[d], recv_sem=st_r.at[d],
            device_id=(speer(d), t), device_id_type=MESH,
        )

    order = (4, 3, 5, 2, 6, 1, 7)
    for d in order:
        zk_copy(d).start()

    wcopy(0).wait()
    queries = jnp.dot(normed, wqkv[0], preferred_element_type=F32).astype(BF16).astype(F32) * 0.125
    low32 = lane_iota(32) < 64
    for j in range(4):
        q2 = queries[:, 128 * j : 128 * j + 128]
        a, b = q2[0:32], q2[32:64]
        sb[2 * j, 64:96, :] = jnp.where(low32, a, swap_halves(b)).astype(BF16)
        sb[2 * j + 1, 64:96, :] = jnp.where(low32, swap_halves(a), b).astype(BF16)
    for d in order:
        zq_copy(d).start()

    early = z < 4

    for d in order:
        st_copy(d).start()


    own_kv = pltpu.make_async_copy(
        sb.at[z, pl.ds(0, 64)], kvb.at[y, c, pl.ds(pl.multiple_of(z * 64, 64), 64)], zk_r.at[z]
    )
    own_kv.start()
    own_q = pltpu.make_async_copy(sb.at[z, pl.ds(64, 32)], qb.at[z], zq_r.at[z])
    own_q.start()
    rst[s] = sb[s]
    group = lax.div(lax.broadcasted_iota(jnp.int32, (8, 512), 1), 64)
    for yy in range(4):
        row = jnp.zeros((8, 512), F32)
        for zz in range(8):
            bias = jnp.where(act_ref[0, zz * 4 + yy] > 0, 0.0, NEG).astype(F32)
            row = jnp.where(group == zz, bias, row)
        biasb[yy] = row
    for j in range(4):
        q2 = queries[:, 128 * j : 128 * j + 128]
        k2 = keys[:, 128 * j : 128 * j + 128].astype(BF16).astype(F32)
        prod = q2 * k2
        even = jnp.sum(jnp.where(low, prod, 0.0), axis=1, keepdims=True)
        odd = jnp.sum(jnp.where(low, 0.0, prod), axis=1, keepdims=True)
        selfm[2 * j] = jnp.broadcast_to(even, (FR, LANES))
        selfm[2 * j + 1] = jnp.broadcast_to(odd, (FR, LANES))

    def zk_wait(zz):
        block = kvb.at[y, c, pl.ds(zz * 64, 64)]
        pltpu.make_async_copy(block, block, zk_r.at[zz]).wait()

    def zq_wait(zz):
        pltpu.make_async_copy(qb.at[zz], qb.at[zz], zq_r.at[zz]).wait()

    def part(yy, cc, g):
        return kvb.at[yy, cc, pl.ds(g * HALF, HALF)]

    held = (y, y1, far_inner, jnp.where(inner, 3 - y1, 0))

    def c_copy(i, g):
        return pltpu.make_async_remote_copy(
            src_ref=part(held[i], c, g), dst_ref=part(held[i], c, g),
            send_sem=c_s.at[4 * g + i], recv_sem=c_r.at[4 * g + i], device_id=core, device_id_type=MESH,
        )

    def c_arrival(i, g):
        return pltpu.make_async_remote_copy(
            src_ref=part(held[i], 1 - c, g), dst_ref=part(held[i], 1 - c, g),
            send_sem=c_s.at[4 * g + i], recv_sem=c_r.at[4 * g + i], device_id=core, device_id_type=MESH,
        )

    def y_copy(block, target, ssem, rsem, g):
        return pltpu.make_async_remote_copy(
            src_ref=part(block, c, g), dst_ref=part(block, c, g),
            send_sem=ssem, recv_sem=rsem, device_id=at(z, target, c), device_id_type=MESH,
        )

    def send_near(g):
        return y_copy(y, y1, y_s.at[2 * g], y_r.at[3 * g], g)

    def send_far(g):
        return y_copy(y, far_inner, y_s.at[2 * g + 1], y_r.at[3 * g + 1], g)

    def onward(g):
        return y_copy(y1, far_inner, f_s.at[g], y_r.at[3 * g + 2], g)

    def lend_queries():
        return pltpu.make_async_remote_copy(
            src_ref=qb, dst_ref=qo, send_sem=o_s, recv_sem=o_r,
            device_id=at(z, y1, c), device_id_type=MESH,
        )

    def gather_z(g):
        for zz in range(4 * g, 4 * g + 4):
            zk_wait(zz)

        @pl.when(inner)
        def _():
            send_far(g).start()

        send_near(g).start()
        c_copy(0, g).start()

    def gather_near(g):
        y_copy(y1, y1, y_s.at[2 * g], y_r.at[3 * g], g).wait_recv()

        @pl.when(inner)
        def _():
            onward(g).start()

        c_copy(1, g).start()

    def gather_far(i, g):
        y_copy(held[i], far_inner, f_s.at[g], y_r.at[3 * g + i - 1], g).wait_recv()
        c_copy(i, g).start()

    def gather_core(i):
        for g in range(2):
            c_arrival(i, g).wait_recv()

    def unfold(source, target):
        for zz in range(8):
            f = source[zz].astype(F32)
            target[zz * 64 : zz * 64 + 32, :] = unfold_low(f)
            target[zz * 64 + 32 : zz * 64 + 64, :] = unfold_high(f)

    def cell(queries_ref, g, which, old=None):
        rows = slice(g * HALF, g * HALF + HALF)
        keys_at = [(2 * which + i, cc) for i in range(2) for cc in range(2)]
        zq = queries_ref[rows, :]
        top = None
        for b, (yy, cc) in enumerate(keys_at):
            sc = nt_dot(zq, kvb[yy, cc]) + biasb[yy, 0:1, :]
            scb[g, :, 512 * b : 512 * b + 512] = sc
            for k in range(0, 512, LANES):
                one = sc[:, k : k + LANES]
                top = one if top is None else jnp.maximum(top, one)
        m = jnp.broadcast_to(jnp.max(top, axis=1, keepdims=True), (HALF, LANES))
        if old is not None:
            m = jnp.maximum(old[0], m)
        total = None
        for b, (yy, cc) in enumerate(keys_at):
            p = jnp.exp2((scb[g, :, 512 * b : 512 * b + 512] - m[:, 0:1]) * LOG2E).astype(BF16)
            new = jnp.dot(p, ones_values(kvb[yy, cc]), preferred_element_type=F32)
            total = new if total is None else total + new
        if old is not None:
            total = old[1] * jnp.exp2((old[0] - m) * LOG2E) + total
        return m, total

    def kept(g):
        rows = slice(g * HALF, g * HALF + HALF)
        return mb[rows, :], accb[rows, :]

    def tb_copy(zz):
        return pltpu.make_async_remote_copy(
            src_ref=ob.at[zz], dst_ref=rt.at[z],
            send_sem=tb_s.at[zz], recv_sem=tb_r.at[z],
            device_id=at(zz, y, c), device_id_type=MESH,
        )

    def tu_copy(zz):
        return pltpu.make_async_remote_copy(
            src_ref=oo.at[zz], dst_ref=ro.at[z],
            send_sem=u_s.at[zz], recv_sem=u_r.at[z],
            device_id=at(zz, y1, c), device_id_type=MESH,
        )

    def give_lent(g, m, total):
        packed = pack_part(m, total)
        for k in range(4):
            zz = 4 * g + k
            oo[zz] = packed[64 * k : 64 * k + 64, :]
            tu_copy(zz).start()

    def give_back(g, m, total):
        packed = pack_part(m, total)
        for k in range(4):
            zz = 4 * g + k
            ob[zz] = packed[64 * k : 64 * k + 64, :]

            @pl.when(z != zz)
            def _():
                tb_copy(zz).start()

            @pl.when(z == zz)
            def _():
                pltpu.make_async_copy(ob.at[zz], rt.at[zz], tb_r.at[zz]).start()

    def sb_copy(d):
        return pltpu.make_async_remote_copy(
            src_ref=so.at[speer(d)], dst_ref=rs.at[s],
            send_sem=sb_s.at[d], recv_sem=sb_r.at[d],
            device_id=(speer(d), t), device_id_type=MESH,
        )

    def across_stems():
        for d in order[::-1]:
            st_copy(d).wait_recv()
        row = lax.broadcasted_iota(jnp.int32, (LANES, LANES), 0)
        col = lax.broadcasted_iota(jnp.int32, (LANES, LANES), 1)
        keep = jnp.logical_and(jnp.bitwise_and(row, 15) == jnp.bitwise_and(col, 15), row != col)
        for f0 in range(0, FR, 16):
            q0 = 64 + f0 % 32
            folded = jnp.concatenate([rst[ss, q0 : q0 + 16, :] for ss in range(8)], axis=0).astype(F32)
            qst = unfold_low(folded) if f0 < 32 else unfold_high(folded)
            kvst = jnp.concatenate([rst[ss, f0 : f0 + 16, :] for ss in range(8)], axis=0)
            sc = jnp.where(keep, nt_dot(qst, kvst), NEG)
            top = jnp.max(sc, axis=1, keepdims=True)
            p = jnp.exp2((sc - top) * LOG2E).astype(BF16)
            done = pack_part(top, jnp.dot(p, ones_values(kvst), preferred_element_type=F32))
            for ss in range(8):
                so[ss, f0 : f0 + 16, :] = done[16 * ss : 16 * ss + 16, :]
        for d in order:
            sb_copy(d).start()
        rs[s] = so[s]

    gather_z(0)
    gather_z(1)
    for zz in range(8):
        zq_wait(zz)

    @pl.when(outer)
    def _():
        lend_queries().start()

    unfold(qb, zb)
    for g in range(2):
        gather_near(g)


    @pl.when(inner)
    def _():
        for g in range(2):
            gather_far(2, g)
        lend_queries().wait_recv()
        unfold(qo, zo)

    @pl.when(early)
    def _():
        across_stems()

    gather_core(0)
    gather_core(1)
    for g in range(2):
        m, total = cell(zb, g, pair)
        mb[g * HALF : g * HALF + HALF, :] = m
        accb[g * HALF : g * HALF + HALF, :] = total

    @pl.when(outer)
    def _():
        for g in range(2):
            give_back(g, *kept(g))

    @pl.when(inner)
    def _():
        for g in range(2):
            gather_far(3, g)

    @pl.when(inner)
    def _():
        gather_core(2)
        gather_core(3)
        for g in range(2):
            give_lent(g, *cell(zo, g, 1 - pair))
            give_back(g, *cell(zb, g, 1 - pair, kept(g)))

    @pl.when(jnp.logical_not(early))
    def _():
        across_stems()

    for d in order[::-1]:
        sb_copy(d).wait_recv()
    for zz in range(8):
        pltpu.make_async_copy(rt.at[zz], rt.at[zz], tb_r.at[zz]).wait()

    @pl.when(outer)
    def _():
        for zz in range(8):
            pltpu.make_async_copy(ro.at[zz], ro.at[zz], u_r.at[zz]).wait()

    @pl.when(inner)
    def _():
        ro[...] = jnp.full((8, FR, LANES), NEG, BF16)

    own = act_ref[0, z * 4 + y] > 0
    halves = []
    for h in range(8):
        a = rs[h].astype(F32)
        b = rt[h].astype(F32)
        la = unpack_lse(a)
        lb = jnp.where(own, unpack_lse(b), selfm[h, :, 0:1])
        b = jnp.where(own, b, sb[h, 0:64, :].astype(F32))
        e = ro[h].astype(F32)
        le = jnp.where(own, unpack_lse(e), NEG)
        m = jnp.maximum(jnp.maximum(la, lb), le)
        wa = jnp.exp2((la - m) * LOG2E)
        wb = jnp.exp2((lb - m) * LOG2E)
        we = jnp.exp2((le - m) * LOG2E)
        inv = 1.0 / (wa + wb + we)
        halves.append(a * (wa * inv) + b * (wb * inv) + e * (we * inv))
    pairs = [
        jnp.where(low, swap_halves(halves[2 * j]), halves[2 * j + 1]).astype(BF16) for j in range(4)
    ]
    attended = jnp.concatenate(pairs, axis=1)
    wcopy(3).wait()
    branch = jnp.dot(attended, wout[...], preferred_element_type=F32)
    out_ref[...] = (resid[...] + ada_row(2) * branch).astype(BF16)

    for d in order:
        zk_copy(d).wait_send()
        zq_copy(d).wait_send()
        st_copy(d).wait_send()
        sb_copy(d).wait_send()
    for zz in range(8):
        @pl.when(z != zz)
        def _():
            tb_copy(zz).wait_send()
    for g in range(2):
        send_near(g).wait_send()
        c_copy(0, g).wait_send()
        c_copy(1, g).wait_send()

    @pl.when(outer)
    def _():
        lend_queries().wait_send()

    @pl.when(inner)
    def _():
        for g in range(2):
            send_far(g).wait_send()
            onward(g).wait_send()
            c_copy(2, g).wait_send()
            c_copy(3, g).wait_send()
        for zz in range(8):
            tu_copy(zz).wait_send()


def body(hidden, control_ids, control_table, activity, ada, w_qkv, w_out):
    vmem = pl.BlockSpec(memory_space=pltpu.VMEM)
    anywhere = pl.BlockSpec(memory_space=pl.ANY)
    dma = pltpu.SemaphoreType.DMA
    out = pl.pallas_call(
        kernel,
        name="attention_block",
        out_shape=jax.ShapeDtypeStruct((FR, 1024), BF16),
        in_specs=[anywhere] * 7,
        out_specs=vmem,
        scratch_shapes=[
            pltpu.VMEM((FR, 1024), BF16),
            pltpu.VMEM((1, FR), jnp.int32),
            pltpu.VMEM((128, 1024), BF16),
            pltpu.SMEM((1, 32), jnp.int32),
            pltpu.VMEM((24, LANES), F32),
            pltpu.VMEM((3, 1024, 512), BF16),
            pltpu.VMEM((512, 1024), BF16),
            pltpu.VMEM((FR, 1024), F32),
            pltpu.VMEM((8, 96, LANES), BF16),
            pltpu.VMEM((4, 2, 512, LANES), BF16),
            pltpu.VMEM((8, 32, LANES), BF16),
            pltpu.VMEM((8, 32, LANES), BF16),
            pltpu.VMEM((512, LANES), BF16),
            pltpu.VMEM((512, LANES), BF16),
            pltpu.VMEM((8, 96, LANES), BF16),
            pltpu.VMEM((2, HALF, 8 * HALF), F32),
            pltpu.VMEM((512, LANES), F32),
            pltpu.VMEM((512, LANES), F32),
            pltpu.VMEM((4, 8, 512), F32),
            pltpu.VMEM((8, FR, LANES), F32),
            pltpu.VMEM((8, FR, LANES), BF16),
            pltpu.VMEM((8, FR, LANES), BF16),
            pltpu.VMEM((8, FR, LANES), BF16),
            pltpu.VMEM((8, FR, LANES), BF16),
            pltpu.VMEM((8, FR, LANES), BF16),
            pltpu.VMEM((8, FR, LANES), BF16),
            dma((5,)),
            dma((4,)),
            dma((8,)), dma((8,)), dma((8,)), dma((8,)), dma((8,)), dma((8,)),
            dma((4,)), dma((6,)), dma((2,)), dma((8,)), dma((8,)), dma, dma, dma((8,)), dma((8,)),
            dma((8,)), dma((8,)), dma((8,)), dma((8,)),
        ],
        compiler_params=pltpu.CompilerParams(
            collective_id=0, has_side_effects=True, vmem_limit_bytes=60 * 1024 * 1024
        ),
    )(hidden[0], control_ids[None, :], control_table, activity, ada.reshape(24, LANES), w_qkv, w_out)
    return out[None]


def solution(mesh):
    placed = (P("stem", "tm", None), P("tm"), P(), P("stem", None), P("stem", None, None), P(), P())
    return jax.shard_map(
        body, mesh=mesh, in_specs=placed, out_specs=P("stem", "tm", None), check_vma=False
    )
```

```python
import functools
import math

import jax
import jax.numpy as jnp
from jax import lax
from jax.experimental import pallas as pl
from jax.experimental.pallas import tpu as pltpu
from jax.sharding import PartitionSpec as P

MESH = pl.DeviceIdType.MESH
F32 = jnp.float32
BF16 = jnp.bfloat16
LOG2E = math.log2(math.e)
NEG = -1e30
FR = 64
LANES = 128
HALF = 256


def lane_iota(rows):
    return lax.broadcasted_iota(jnp.int32, (rows, LANES), 1)


def swap_halves(x):
    return pltpu.roll(x, 64, 1)


def nt_dot(a, b):
    return lax.dot_general(a, b, (((1,), (1,)), ((), ())), preferred_element_type=F32)


def unfold_low(f):
    return jnp.where(lane_iota(f.shape[0]) < 64, f, 0.0).astype(BF16)


def unfold_high(f):
    return unfold_low(swap_halves(f))


def ones_values(kv):
    return jnp.where(lane_iota(kv.shape[0]) < 64, jnp.ones_like(kv), kv)


def pack_part(m, acc):
    rows = acc.shape[0]
    lane = lane_iota(rows)
    total = jnp.where(lane < 64, acc, swap_halves(acc))
    value = acc / total
    lse = m + jnp.log(total)
    hi = lse.astype(BF16).astype(F32)
    mid = (lse - hi).astype(BF16).astype(F32)
    lo = lse - hi - mid
    return jnp.where(
        lane < 16, hi, jnp.where(lane < 32, mid, jnp.where(lane < 64, lo, value))
    ).astype(BF16)


def unpack_lse(part):
    return part[:, 0:1] + part[:, 16:17] + part[:, 32:33]


def kernel(
    hidden_hbm, ids_hbm, table_hbm, act_hbm, ada_hbm, wqkv_hbm, wout_hbm, out_ref,
    hidden_ref, ids_ref, table_ref, act_ref, ada_ref,
    wqkv, wout, resid, sb, kvb, qb, qo, zb, zo, rst, scb, mb, accb, biasb, selfm, ob, oo, so, rt, ro, rs,
    i_sem, w_sem, zk_s, zk_r, zq_s, zq_r, st_s, st_r, y_s, y_r, f_s, c_s, c_r, o_s, o_r, u_s, u_r, tb_s, tb_r, sb_s, sb_r,
):
    s = lax.axis_index("stem")
    t = lax.axis_index("tm")
    z = lax.div(t, 8)
    y = lax.rem(lax.div(t, 2), 4)
    c = lax.rem(t, 2)
    y1 = y + 1 - 2 * lax.rem(y, 2)
    inner = jnp.logical_or(y == 1, y == 2)
    outer = jnp.logical_not(inner)
    far_inner = 3 - y
    pair = lax.div(y, 2)

    def at(zz, yy, cc):
        return (s, (zz * 4 + yy) * 2 + cc)

    def zpeer(d):
        return lax.rem(z + d, 8)

    def speer(d):
        return lax.rem(s + d, 8)

    core = at(z, y, 1 - c)

    barrier = pltpu.get_barrier_semaphore()
    for d in range(1, 8):
        pl.semaphore_signal(barrier, inc=1, device_id=at(zpeer(d), y, c), device_id_type=MESH)
        pl.semaphore_signal(barrier, inc=1, device_id=(speer(d), t), device_id_type=MESH)
    pl.semaphore_signal(barrier, inc=1, device_id=at(z, y1, c), device_id_type=MESH)

    @pl.when(inner)
    def _():
        pl.semaphore_signal(barrier, inc=1, device_id=at(z, far_inner, c), device_id_type=MESH)

    @pl.when(outer)
    def _():
        for d in range(1, 8):
            pl.semaphore_signal(barrier, inc=1, device_id=at(zpeer(d), y1, c), device_id_type=MESH)

    pl.semaphore_signal(barrier, inc=1, device_id=core, device_id_type=MESH)

    def wcopy(i):
        if i == 3:
            return pltpu.make_async_copy(wout_hbm, wout, w_sem.at[3])
        cols = pl.ds(i * 512, 512)
        return pltpu.make_async_copy(wqkv_hbm.at[:, cols], wqkv.at[i], w_sem.at[i])

    small = [
        pltpu.make_async_copy(src, dst, i_sem.at[n])
        for n, (src, dst) in enumerate(
            (
                (hidden_hbm, hidden_ref), (ids_hbm, ids_ref), (table_hbm, table_ref),
                (ada_hbm, ada_ref), (act_hbm, act_ref),
            )
        )
    ]
    for copy in small:
        copy.start()
    for i in (1, 2, 0, 3):
        wcopy(i).start()
    for copy in small:
        copy.wait()

    def ada_row(i):
        return jnp.concatenate([ada_ref[8 * i + k : 8 * i + k + 1, :] for k in range(8)], axis=1)

    onehot = (lax.broadcasted_iota(jnp.int32, (128, FR), 0) == ids_ref[...]).astype(BF16)
    lookup = lax.dot_general(
        onehot, table_ref[...], (((0,), (0,)), ((), ())), preferred_element_type=F32
    )
    residual = hidden_ref[...].astype(F32) + lookup
    resid[...] = residual
    mean = jnp.mean(residual, axis=-1, keepdims=True)
    cent = residual - mean
    var = jnp.mean(jnp.square(cent), axis=-1, keepdims=True)
    normed = (cent * lax.rsqrt(var + 1e-6) * (1.0 + ada_row(1)) + ada_row(0)).astype(BF16)

    low = lane_iota(FR) < 64
    wcopy(1).wait()
    keys = jnp.dot(normed, wqkv[1], preferred_element_type=F32)
    wcopy(2).wait()
    values = jnp.dot(normed, wqkv[2], preferred_element_type=F32)
    for j in range(4):
        k2 = keys[:, 128 * j : 128 * j + 128]
        v2 = values[:, 128 * j : 128 * j + 128]
        sb[2 * j, 0:64, :] = jnp.where(low, k2, swap_halves(v2)).astype(BF16)
        sb[2 * j + 1, 0:64, :] = jnp.where(low, swap_halves(k2), v2).astype(BF16)

    pl.semaphore_wait(barrier, jnp.where(inner, 24, 16))

    def zk_copy(d):
        return pltpu.make_async_remote_copy(
            src_ref=sb.at[zpeer(d), pl.ds(0, 64)],
            dst_ref=kvb.at[y, c, pl.ds(pl.multiple_of(z * 64, 64), 64)],
            send_sem=zk_s.at[d], recv_sem=zk_r.at[z],
            device_id=at(zpeer(d), y, c), device_id_type=MESH,
        )

    def zq_copy(d):
        return pltpu.make_async_remote_copy(
            src_ref=sb.at[zpeer(d), pl.ds(64, 32)],
            dst_ref=qb.at[z],
            send_sem=zq_s.at[d], recv_sem=zq_r.at[z],
            device_id=at(zpeer(d), y, c), device_id_type=MESH,
        )

    def st_copy(d):
        return pltpu.make_async_remote_copy(
            src_ref=sb.at[speer(d)], dst_ref=rst.at[s],
            send_sem=st_s.at[d], recv_sem=st_r.at[d],
            device_id=(speer(d), t), device_id_type=MESH,
        )

    order = (4, 3, 5, 2, 6, 1, 7)
    for d in order:
        zk_copy(d).start()

    wcopy(0).wait()
    queries = jnp.dot(normed, wqkv[0], preferred_element_type=F32).astype(BF16).astype(F32) * 0.125
    low32 = lane_iota(32) < 64
    for j in range(4):
        q2 = queries[:, 128 * j : 128 * j + 128]
        a, b = q2[0:32], q2[32:64]
        sb[2 * j, 64:96, :] = jnp.where(low32, a, swap_halves(b)).astype(BF16)
        sb[2 * j + 1, 64:96, :] = jnp.where(low32, swap_halves(a), b).astype(BF16)
    for d in order:
        zq_copy(d).start()

    early = z < 4

    for d in order:
        st_copy(d).start()


    own_kv = pltpu.make_async_copy(
        sb.at[z, pl.ds(0, 64)], kvb.at[y, c, pl.ds(pl.multiple_of(z * 64, 64), 64)], zk_r.at[z]
    )
    own_kv.start()
    own_q = pltpu.make_async_copy(sb.at[z, pl.ds(64, 32)], qb.at[z], zq_r.at[z])
    own_q.start()
    rst[s] = sb[s]
    group = lax.div(lax.broadcasted_iota(jnp.int32, (8, 512), 1), 64)
    for yy in range(4):
        row = jnp.zeros((8, 512), F32)
        for zz in range(8):
            bias = jnp.where(act_ref[0, zz * 4 + yy] > 0, 0.0, NEG).astype(F32)
            row = jnp.where(group == zz, bias, row)
        biasb[yy] = row
    for j in range(4):
        q2 = queries[:, 128 * j : 128 * j + 128]
        k2 = keys[:, 128 * j : 128 * j + 128].astype(BF16).astype(F32)
        prod = q2 * k2
        even = jnp.sum(jnp.where(low, prod, 0.0), axis=1, keepdims=True)
        odd = jnp.sum(jnp.where(low, 0.0, prod), axis=1, keepdims=True)
        selfm[2 * j] = jnp.broadcast_to(even, (FR, LANES))
        selfm[2 * j + 1] = jnp.broadcast_to(odd, (FR, LANES))

    def zk_wait(zz):
        block = kvb.at[y, c, pl.ds(zz * 64, 64)]
        pltpu.make_async_copy(block, block, zk_r.at[zz]).wait()

    def zq_wait(zz):
        pltpu.make_async_copy(qb.at[zz], qb.at[zz], zq_r.at[zz]).wait()

    def part(yy, cc, g):
        return kvb.at[yy, cc, pl.ds(g * HALF, HALF)]

    held = (y, y1, far_inner, jnp.where(inner, 3 - y1, 0))

    def c_copy(i, g):
        return pltpu.make_async_remote_copy(
            src_ref=part(held[i], c, g), dst_ref=part(held[i], c, g),
            send_sem=c_s.at[4 * g + i], recv_sem=c_r.at[4 * g + i], device_id=core, device_id_type=MESH,
        )

    def c_arrival(i, g):
        return pltpu.make_async_remote_copy(
            src_ref=part(held[i], 1 - c, g), dst_ref=part(held[i], 1 - c, g),
            send_sem=c_s.at[4 * g + i], recv_sem=c_r.at[4 * g + i], device_id=core, device_id_type=MESH,
        )

    def y_copy(block, target, ssem, rsem, g):
        return pltpu.make_async_remote_copy(
            src_ref=part(block, c, g), dst_ref=part(block, c, g),
            send_sem=ssem, recv_sem=rsem, device_id=at(z, target, c), device_id_type=MESH,
        )

    def send_near(g):
        return y_copy(y, y1, y_s.at[2 * g], y_r.at[3 * g], g)

    def send_far(g):
        return y_copy(y, far_inner, y_s.at[2 * g + 1], y_r.at[3 * g + 1], g)

    def onward(g):
        return y_copy(y1, far_inner, f_s.at[g], y_r.at[3 * g + 2], g)

    def lend_queries():
        return pltpu.make_async_remote_copy(
            src_ref=qb, dst_ref=qo, send_sem=o_s, recv_sem=o_r,
            device_id=at(z, y1, c), device_id_type=MESH,
        )

    def gather_z(g):
        for zz in range(4 * g, 4 * g + 4):
            zk_wait(zz)

        @pl.when(inner)
        def _():
            send_far(g).start()

        send_near(g).start()
        c_copy(0, g).start()

    def gather_near(g):
        y_copy(y1, y1, y_s.at[2 * g], y_r.at[3 * g], g).wait_recv()

        @pl.when(inner)
        def _():
            onward(g).start()

        c_copy(1, g).start()

    def gather_far(i, g):
        y_copy(held[i], far_inner, f_s.at[g], y_r.at[3 * g + i - 1], g).wait_recv()
        c_copy(i, g).start()

    def gather_core(i):
        for g in range(2):
            c_arrival(i, g).wait_recv()

    def unfold(source, target):
        for zz in range(8):
            f = source[zz].astype(F32)
            target[zz * 64 : zz * 64 + 32, :] = unfold_low(f)
            target[zz * 64 + 32 : zz * 64 + 64, :] = unfold_high(f)

    def cell(queries_ref, g, which, old=None):
        rows = slice(g * HALF, g * HALF + HALF)
        keys_at = [(2 * which + i, cc) for i in range(2) for cc in range(2)]
        zq = queries_ref[rows, :]
        top = None
        for b, (yy, cc) in enumerate(keys_at):
            sc = nt_dot(zq, kvb[yy, cc]) + biasb[yy, 0:1, :]
            scb[g, :, 512 * b : 512 * b + 512] = sc
            for k in range(0, 512, LANES):
                one = sc[:, k : k + LANES]
                top = one if top is None else jnp.maximum(top, one)
        m = jnp.broadcast_to(jnp.max(top, axis=1, keepdims=True), (HALF, LANES))
        if old is not None:
            m = jnp.maximum(old[0], m)
        total = None
        for b, (yy, cc) in enumerate(keys_at):
            p = jnp.exp2((scb[g, :, 512 * b : 512 * b + 512] - m[:, 0:1]) * LOG2E).astype(BF16)
            new = jnp.dot(p, ones_values(kvb[yy, cc]), preferred_element_type=F32)
            total = new if total is None else total + new
        if old is not None:
            total = old[1] * jnp.exp2((old[0] - m) * LOG2E) + total
        return m, total

    def kept(g):
        rows = slice(g * HALF, g * HALF + HALF)
        return mb[rows, :], accb[rows, :]

    def tb_copy(zz):
        return pltpu.make_async_remote_copy(
            src_ref=ob.at[zz], dst_ref=rt.at[z],
            send_sem=tb_s.at[zz], recv_sem=tb_r.at[z],
            device_id=at(zz, y, c), device_id_type=MESH,
        )

    def tu_copy(zz):
        return pltpu.make_async_remote_copy(
            src_ref=oo.at[zz], dst_ref=ro.at[z],
            send_sem=u_s.at[zz], recv_sem=u_r.at[z],
            device_id=at(zz, y1, c), device_id_type=MESH,
        )

    def give_lent(g, m, total):
        packed = pack_part(m, total)
        for k in range(4):
            zz = 4 * g + k
            oo[zz] = packed[64 * k : 64 * k + 64, :]
            tu_copy(zz).start()

    def give_back(g, m, total):
        packed = pack_part(m, total)
        for k in range(4):
            zz = 4 * g + k
            ob[zz] = packed[64 * k : 64 * k + 64, :]

            @pl.when(z != zz)
            def _():
                tb_copy(zz).start()

            @pl.when(z == zz)
            def _():
                pltpu.make_async_copy(ob.at[zz], rt.at[zz], tb_r.at[zz]).start()

    def sb_copy(d):
        return pltpu.make_async_remote_copy(
            src_ref=so.at[speer(d)], dst_ref=rs.at[s],
            send_sem=sb_s.at[d], recv_sem=sb_r.at[d],
            device_id=(speer(d), t), device_id_type=MESH,
        )

    def across_stems():
        for d in order[::-1]:
            st_copy(d).wait_recv()
        row = lax.broadcasted_iota(jnp.int32, (LANES, LANES), 0)
        col = lax.broadcasted_iota(jnp.int32, (LANES, LANES), 1)
        keep = jnp.logical_and(jnp.bitwise_and(row, 15) == jnp.bitwise_and(col, 15), row != col)
        for f0 in range(0, FR, 16):
            q0 = 64 + f0 % 32
            folded = jnp.concatenate([rst[ss, q0 : q0 + 16, :] for ss in range(8)], axis=0).astype(F32)
            qst = unfold_low(folded) if f0 < 32 else unfold_high(folded)
            kvst = jnp.concatenate([rst[ss, f0 : f0 + 16, :] for ss in range(8)], axis=0)
            sc = jnp.where(keep, nt_dot(qst, kvst), NEG)
            top = jnp.max(sc, axis=1, keepdims=True)
            p = jnp.exp2((sc - top) * LOG2E).astype(BF16)
            done = pack_part(top, jnp.dot(p, ones_values(kvst), preferred_element_type=F32))
            for ss in range(8):
                so[ss, f0 : f0 + 16, :] = done[16 * ss : 16 * ss + 16, :]
        for d in order:
            sb_copy(d).start()
        rs[s] = so[s]

    gather_z(0)
    gather_z(1)
    for zz in range(8):
        zq_wait(zz)

    @pl.when(outer)
    def _():
        lend_queries().start()

    unfold(qb, zb)
    for g in range(2):
        gather_near(g)


    @pl.when(inner)
    def _():
        for g in range(2):
            gather_far(2, g)

    @pl.when(early)
    def _():
        across_stems()

    gather_core(0)
    gather_core(1)
    for g in range(2):
        m, total = cell(zb, g, pair)
        mb[g * HALF : g * HALF + HALF, :] = m
        accb[g * HALF : g * HALF + HALF, :] = total

    @pl.when(outer)
    def _():
        for g in range(2):
            give_back(g, *kept(g))

    @pl.when(inner)
    def _():
        for g in range(2):
            gather_far(3, g)

    @pl.when(inner)
    def _():
        lend_queries().wait_recv()
        unfold(qo, zo)
        gather_core(2)
        gather_core(3)
        for g in range(2):
            give_lent(g, *cell(zo, g, 1 - pair))
            give_back(g, *cell(zb, g, 1 - pair, kept(g)))

    @pl.when(jnp.logical_not(early))
    def _():
        across_stems()

    for d in order[::-1]:
        sb_copy(d).wait_recv()
    for zz in range(8):
        pltpu.make_async_copy(rt.at[zz], rt.at[zz], tb_r.at[zz]).wait()

    @pl.when(outer)
    def _():
        for zz in range(8):
            pltpu.make_async_copy(ro.at[zz], ro.at[zz], u_r.at[zz]).wait()

    @pl.when(inner)
    def _():
        ro[...] = jnp.full((8, FR, LANES), NEG, BF16)

    own = act_ref[0, z * 4 + y] > 0
    halves = []
    for h in range(8):
        a = rs[h].astype(F32)
        b = rt[h].astype(F32)
        la = unpack_lse(a)
        lb = jnp.where(own, unpack_lse(b), selfm[h, :, 0:1])
        b = jnp.where(own, b, sb[h, 0:64, :].astype(F32))
        e = ro[h].astype(F32)
        le = jnp.where(own, unpack_lse(e), NEG)
        m = jnp.maximum(jnp.maximum(la, lb), le)
        wa = jnp.exp2((la - m) * LOG2E)
        wb = jnp.exp2((lb - m) * LOG2E)
        we = jnp.exp2((le - m) * LOG2E)
        inv = 1.0 / (wa + wb + we)
        halves.append(a * (wa * inv) + b * (wb * inv) + e * (we * inv))
    pairs = [
        jnp.where(low, swap_halves(halves[2 * j]), halves[2 * j + 1]).astype(BF16) for j in range(4)
    ]
    attended = jnp.concatenate(pairs, axis=1)
    wcopy(3).wait()
    branch = jnp.dot(attended, wout[...], preferred_element_type=F32)
    out_ref[...] = (resid[...] + ada_row(2) * branch).astype(BF16)

    for d in order:
        zk_copy(d).wait_send()
        zq_copy(d).wait_send()
        st_copy(d).wait_send()
        sb_copy(d).wait_send()
    for zz in range(8):
        @pl.when(z != zz)
        def _():
            tb_copy(zz).wait_send()
    for g in range(2):
        send_near(g).wait_send()
        c_copy(0, g).wait_send()
        c_copy(1, g).wait_send()

    @pl.when(outer)
    def _():
        lend_queries().wait_send()

    @pl.when(inner)
    def _():
        for g in range(2):
            send_far(g).wait_send()
            onward(g).wait_send()
            c_copy(2, g).wait_send()
            c_copy(3, g).wait_send()
        for zz in range(8):
            tu_copy(zz).wait_send()


def body(hidden, control_ids, control_table, activity, ada, w_qkv, w_out):
    vmem = pl.BlockSpec(memory_space=pltpu.VMEM)
    anywhere = pl.BlockSpec(memory_space=pl.ANY)
    dma = pltpu.SemaphoreType.DMA
    out = pl.pallas_call(
        kernel,
        name="attention_block",
        out_shape=jax.ShapeDtypeStruct((FR, 1024), BF16),
        in_specs=[anywhere] * 7,
        out_specs=vmem,
        scratch_shapes=[
            pltpu.VMEM((FR, 1024), BF16),
            pltpu.VMEM((1, FR), jnp.int32),
            pltpu.VMEM((128, 1024), BF16),
            pltpu.SMEM((1, 32), jnp.int32),
            pltpu.VMEM((24, LANES), F32),
            pltpu.VMEM((3, 1024, 512), BF16),
            pltpu.VMEM((512, 1024), BF16),
            pltpu.VMEM((FR, 1024), F32),
            pltpu.VMEM((8, 96, LANES), BF16),
            pltpu.VMEM((4, 2, 512, LANES), BF16),
            pltpu.VMEM((8, 32, LANES), BF16),
            pltpu.VMEM((8, 32, LANES), BF16),
            pltpu.VMEM((512, LANES), BF16),
            pltpu.VMEM((512, LANES), BF16),
            pltpu.VMEM((8, 96, LANES), BF16),
            pltpu.VMEM((2, HALF, 8 * HALF), F32),
            pltpu.VMEM((512, LANES), F32),
            pltpu.VMEM((512, LANES), F32),
            pltpu.VMEM((4, 8, 512), F32),
            pltpu.VMEM((8, FR, LANES), F32),
            pltpu.VMEM((8, FR, LANES), BF16),
            pltpu.VMEM((8, FR, LANES), BF16),
            pltpu.VMEM((8, FR, LANES), BF16),
            pltpu.VMEM((8, FR, LANES), BF16),
            pltpu.VMEM((8, FR, LANES), BF16),
            pltpu.VMEM((8, FR, LANES), BF16),
            dma((5,)),
            dma((4,)),
            dma((8,)), dma((8,)), dma((8,)), dma((8,)), dma((8,)), dma((8,)),
            dma((4,)), dma((6,)), dma((2,)), dma((8,)), dma((8,)), dma, dma, dma((8,)), dma((8,)),
            dma((8,)), dma((8,)), dma((8,)), dma((8,)),
        ],
        compiler_params=pltpu.CompilerParams(
            collective_id=0, has_side_effects=True, vmem_limit_bytes=60 * 1024 * 1024
        ),
    )(hidden[0], control_ids[None, :], control_table, activity, ada.reshape(24, LANES), w_qkv, w_out)
    return out[None]


def solution(mesh):
    placed = (P("stem", "tm", None), P("tm"), P(), P("stem", None), P("stem", None, None), P(), P())
    return jax.shard_map(
        body, mesh=mesh, in_specs=placed, out_specs=P("stem", "tm", None), check_vma=False
    )
```
